128 devices in a mesh: strip: 8 (over x, core), blk: 16 (over y, z).
Axes of the slice: x: 4, y: 4, z: 4, core: 2. Of those that a mesh axis runs over, the one named last changes fastest.
Arguments:
- krylov_start: float32 [4, 64, 2048], P(None, 'strip', 'blk'), may hold values from -5 to 6
- conductivity: float32 [4, 64, 2048], P(None, 'strip', 'blk'), may hold values from 0.1 to 1
- near_kernel: bfloat16 [6144, 3, 3, 128, 128], P(('strip', 'blk')), may hold values from -0.125 to 0.125
- near_pair: int32 [6144], P(('strip', 'blk')), may hold values from 0 to 71, as said below
- far_right: bfloat16 [128, 128, 32, 3, 128], P(('strip', 'blk')), may hold values from -1 to 1
- far_left: bfloat16 [128, 128, 32, 3, 128], P(('strip', 'blk')), may hold values from -1 to 1
- far_source_row: int32 [128, 128], P(('strip', 'blk')), may hold values from 0 to 7
- far_target_row: int32 [128, 128], P(('strip', 'blk')), may hold values from 0 to 7
Outputs:
- krylov_next: float32 [2, 4, 64, 2048], P(None, None, 'strip', 'blk')
- hessenberg: float32 [5], replicated
The draws below stay inside these ranges and needn't reach their ends.
Inputs may be any that keep to these rules, and one draw needn't show every extreme that they name: `near_pair`: each device's 48 entries are distinct values c = t * 9 + k: local target block row t and neighbour k as in the reference program. How many of them fall in one block row varies from row to row and device to device; a row holds at most 9. `far_source_row`: entry [g, d] belongs to the far pair owned by device g whose target block lies on device d. `far_target_row`: entry [g, d] is the target block row on device d of the far pair owned by g.
All inputs are finite; a program needn't handle non-finite values.
Results may differ from the reference program's by a relative error of at most 0.0022.
Values sent between devices are 32-bit elements; how exact they have to be, the bound alone decides.
No kernel may reach another device: no remote copies, remote signals or barrier semaphores. Data moves between devices by JAX's collectives and lax.ppermute only.
A program may use at most 64 MiB of HBM per device.

```python
import math
import jax
import jax.numpy as jnp
from jax import lax

B = 128
R = 32
NEAR_BLK = 6
CX = 8
NEAR_DEV = 48
NX = 64
NY = 2048
N_STRIP = 8
N_BLK = 16
DEVICES = 128


def draw_near_pair(key, part):
    key = jax.random.fold_in(key, 11)
    keys = jax.random.split(key, DEVICES)
    picked = jax.vmap(lambda single_key: jax.random.permutation(single_key, CX * 9)[:NEAR_BLK * CX])(keys)
    return picked.reshape(-1).astype(jnp.int32)


def draw_krylov_start(key, part):
    key = jax.random.fold_in(key, 31)
    shape = (4, NX, NY)
    noise = jax.random.truncated_normal(key, -5.0, 5.0, shape, jnp.float32)
    offset = 0.5
    return (noise + offset).astype(jnp.float32)


def draw_far_right(key, part):
    key = jax.random.fold_in(key, 23)
    noise_key, level_key = jax.random.split(key)
    shape = (DEVICES, DEVICES, R, 3, B)
    level_shape = (DEVICES, DEVICES, 1, 1, 1)
    noise = jax.random.truncated_normal(noise_key, -6.0, 6.0, shape, jnp.float32)
    level = jnp.exp(jax.random.uniform(level_key, level_shape, jnp.float32, math.log(0.5), math.log(2.0)))
    values = noise / math.sqrt(3.0 * B) + level * (2.0 / (3.0 * B))
    return values.astype(jnp.bfloat16)


def draw_far_left(key, part):
    key = jax.random.fold_in(key, 47)
    noise_key, level_key = jax.random.split(key)
    shape = (DEVICES, DEVICES, R, 3, B)
    level_shape = (DEVICES, DEVICES, 1, 1, 1)
    noise = jax.random.truncated_normal(noise_key, -6.0, 6.0, shape, jnp.float32)
    level = jnp.exp(jax.random.uniform(level_key, level_shape, jnp.float32, math.log(0.5), math.log(2.0)))
    values = noise / math.sqrt(1.0 * R * DEVICES) + level * (0.5 * CX / (1.0 * R * DEVICES))
    return values.astype(jnp.bfloat16)


def set_ends(values, own_key, low, largest):
    dims = values.shape
    index_at = [jax.random.randint(jax.random.fold_in(own_key, axis), (), 0, dims[axis]) for axis in range(len(dims))]
    values = values.at[tuple(index_at)].set(low)
    longest = dims.index(max(dims))
    index_at[longest] = (index_at[longest] + 1) % dims[longest]
    return values.at[tuple(index_at)].set(largest)


def block_levels(stream_key, shape, pieces, least, largest):
    factor_of = 1.0
    for position, blocks in pieces:
        steps = jax.random.uniform(jax.random.fold_in(jax.random.fold_in(stream_key, 6), position), (blocks,), jnp.float32, least / len(pieces), largest / len(pieces))
        factor_of = factor_of * jnp.repeat(jnp.exp(steps), shape[position] // blocks).reshape((-1,) + (1,) * (len(shape) - 1 - position))
    return factor_of


def scatter_about(rng, shape, spread, reach, cuts=(), kind=jnp.bfloat16):
    loudness = block_levels(rng, shape, cuts, -0.22, 0.18) if cuts else 1.0
    values = jax.random.normal(rng, shape, jnp.float32) * spread * loudness
    return jnp.minimum(jnp.maximum(values, -reach), reach).astype(kind)


def setup_inputs(seed: int = 0) -> dict:
    splits = jax.random.split(jax.random.key(seed), 9)
    krylov_start = draw_krylov_start(jax.random.fold_in(splits[8], 71), 0)
    conductivity = jnp.clip(jnp.exp(math.log(1.0) - 2.3025851 * jax.random.uniform(splits[1], (4, NX, NY), jnp.float32) ** block_levels(splits[1], (4, NX, NY), ((1, 8), (2, 16)), -0.2, 0.2)), 0.1, 1.0)
    near_kernel = scatter_about(splits[2], (NEAR_DEV * DEVICES, 3, 3, B, B), (3 * B * NEAR_BLK) ** -0.5, 0.125, ((0, 128),))
    near_pair = draw_near_pair(jax.random.fold_in(splits[8], 71), 0)
    far_right = draw_far_right(jax.random.fold_in(splits[8], 71), 0)
    far_left = draw_far_left(jax.random.fold_in(splits[8], 71), 0)
    far_source_row = set_ends(jax.random.randint(splits[6], (DEVICES, DEVICES), 0, CX), jax.random.fold_in(splits[6], 1), 0, CX - 1).astype(jnp.int32)
    far_target_row = set_ends(jax.random.randint(splits[7], (DEVICES, DEVICES), 0, CX), jax.random.fold_in(splits[7], 1), 0, CX - 1).astype(jnp.int32)
    return dict(krylov_start=krylov_start, conductivity=conductivity, near_kernel=near_kernel, near_pair=near_pair, far_right=far_right, far_left=far_left, far_source_row=far_source_row, far_target_row=far_target_row)


epsilon = 1e-06

def by_device(field):
    comps = field.shape[0]
    shaped = field.reshape(comps, N_STRIP, CX, N_BLK, B)
    return shaped.transpose(1, 3, 0, 2, 4).reshape(N_STRIP * N_BLK, comps, CX, B)

def from_device(blocks):
    comps = blocks.shape[1]
    shaped = blocks.reshape(N_STRIP, N_BLK, comps, CX, B)
    return shaped.transpose(2, 0, 3, 1, 4).reshape(comps, NX, NY)

def near_field(displaced, near_kernel, near_pair):
    padded = jnp.pad(displaced.reshape(3, NX, N_BLK, B), ((0, 0), (1, 1), (1, 1), (0, 0)))
    pair_codes = near_pair.reshape(DEVICES, NEAR_DEV)
    kernels = near_kernel.reshape(DEVICES, NEAR_DEV, 3, 3, B, B)
    owner_ids = jnp.arange(DEVICES, dtype=jnp.int32)
    row_ids = jnp.arange(CX, dtype=jnp.int32)

    def one_owner(slot_data):
        owner_index, codes, kernel_set = slot_data
        target_row = codes // 9
        neighbour = codes % 9
        source_row = owner_index // N_BLK * CX + target_row + neighbour // 3
        source_col = owner_index % N_BLK + neighbour % 3
        sources = padded[:, source_row, source_col, :]
        products = jnp.einsum('pabim,bpm->pai', kernel_set.astype(jnp.float32), sources.astype(jnp.float32), precision=lax.Precision.HIGHEST)
        onehot = (target_row[:, None] == row_ids[None, :]).astype(jnp.float32)
        return jnp.einsum('pt,pai->ati', onehot, products, precision=lax.Precision.HIGHEST)
    return from_device(lax.map(one_owner, (owner_ids, pair_codes, kernels)))

def far_field(displaced, far_right, far_left, far_source_row, far_target_row):
    blocks = by_device(displaced)
    row_ids = jnp.arange(CX, dtype=jnp.int32)

    def one_owner(totals, slot_data):
        own_blocks, source_rows, targets, right_factor, left_factor = slot_data
        sources = jnp.take(own_blocks, source_rows, axis=1)
        coefficient = jnp.einsum('drbm,bdm->dr', right_factor.astype(jnp.float32), sources.astype(jnp.float32), precision=lax.Precision.HIGHEST).astype(jnp.bfloat16)
        pair_result = jnp.einsum('drai,dr->dai', left_factor.astype(jnp.float32), coefficient.astype(jnp.float32), precision=lax.Precision.HIGHEST)
        onehot = (targets[:, None] == row_ids[None, :]).astype(jnp.float32)
        return (totals + jnp.einsum('dk,dai->daki', onehot, pair_result, precision=lax.Precision.HIGHEST), None)
    start_totals = jnp.zeros((DEVICES, 3, CX, B), jnp.float32)
    totals, _ = lax.scan(one_owner, start_totals, (blocks, far_source_row, far_target_row, far_right, far_left))
    return from_device(totals)

def apply_operator(vector, conductivity, near_kernel, near_pair, far_right, far_left, far_source_row, far_target_row):
    displaced = vector[0:3].astype(jnp.bfloat16)
    near_part = near_field(displaced, near_kernel, near_pair)
    far_part = far_field(displaced, far_right, far_left, far_source_row, far_target_row)
    pressure = vector[3]
    padded = jnp.pad(pressure, 1)
    north_side = padded[:-2, 1:-1]
    south_side = padded[2:, 1:-1]
    west_side = padded[1:-1, :-2]
    east_side = padded[1:-1, 2:]
    flux_sum = conductivity[0] * (north_side - pressure) + conductivity[1] * (south_side - pressure)
    flux_sum = flux_sum + conductivity[2] * (west_side - pressure) + conductivity[3] * (east_side - pressure)
    elastic = vector[0:3] + near_part + far_part
    elastic = jnp.concatenate([elastic[0:1] - pressure[None], elastic[1:3]], axis=0)
    fluid = pressure + vector[0] - flux_sum
    return jnp.concatenate([elastic, fluid[None]], axis=0)

def reference(krylov_start, conductivity, near_kernel, near_pair, far_right, far_left, far_source_row, far_target_row):
    entries = 4.0 * NX * NY
    image = apply_operator(krylov_start, conductivity, near_kernel, near_pair, far_right, far_left, far_source_row, far_target_row)
    first_proj = jnp.sum(krylov_start * image) / entries
    remainder = image - first_proj * krylov_start
    first_norm = jnp.sqrt(jnp.sum(remainder * remainder) / entries + epsilon)
    first_vector = remainder / first_norm
    image = apply_operator(first_vector, conductivity, near_kernel, near_pair, far_right, far_left, far_source_row, far_target_row)
    proj_start = jnp.sum(krylov_start * image) / entries
    proj_first = jnp.sum(first_vector * image) / entries
    remainder = image - proj_start * krylov_start - proj_first * first_vector
    second_norm = jnp.sqrt(jnp.sum(remainder * remainder) / entries + epsilon)
    second_vector = remainder / second_norm
    return (jnp.stack([first_vector, second_vector]), jnp.stack([first_proj, first_norm, proj_start, proj_first, second_norm]))
```

```python
import functools

import jax
import jax.numpy as jnp
from jax import lax
from jax.experimental import pallas as pl
from jax.experimental.pallas import tpu as pltpu
from jax.sharding import PartitionSpec as P

EPSILON = 1e-06
STRIPS, BLKS, DEVICES = 8, 16, 128
ROWS, LEN, RANK, PAIRS = 8, 128, 32, 48
ENTRIES = float(4 * STRIPS * ROWS * BLKS * LEN)
HALO = 32
NEAR_CHUNK = 4
NEAR_CHUNKS = PAIRS // NEAR_CHUNK
FAR_CHUNK = 8
FAR_CHUNKS = DEVICES // FAR_CHUNK
FAR_COPIES = 4
FAR_PER_COPY = DEVICES // FAR_COPIES
BF16, F32 = jnp.bfloat16, jnp.float32
TRANS_B = (((1,), (1,)), ((), ()))
PLAIN = (((1,), (0,)), ((), ()))
VMEM = pl.BlockSpec(memory_space=pltpu.VMEM)
SMEM = pl.BlockSpec(memory_space=pltpu.SMEM)
ANY = pl.BlockSpec(memory_space=pl.ANY)


def two_sum(a, b):
    s = a + b
    t = s - a
    return s, (a - (s - t)) + (b - t)


def halves(a):
    c = a * 4097.0
    hi = c - (c - a)
    return hi, a - hi


def two_prod(a, b):
    p = a * b
    ah, al = halves(a)
    bh, bl = halves(b)
    return p, ((ah * bh - p) + ah * bl + al * bh) + al * bl


def pair_add(x, y):
    s, e = two_sum(x[0], y[0])
    return two_sum(s, e + (x[1] + y[1]))


def pair_mul(x, y):
    p, e = two_prod(x[0], y[0])
    return two_sum(p, e + (x[0] * y[1] + x[1] * y[0]))


def neg(x):
    return -x[0], -x[1]


def scaled(x, power_of_two):
    return x[0] * power_of_two, x[1] * power_of_two


def dot_row(pairs):
    sub = lax.broadcasted_iota(jnp.int32, (8, LEN), 0)
    high = jnp.zeros((8, LEN), F32)
    low = jnp.zeros((8, LEN), F32)
    for k, (a, b) in enumerate(pairs):
        s, e = two_prod(a[0], b[0])
        for c in range(1, 4):
            s, e = pair_add((s, e), two_prod(a[c], b[c]))
        for step in (4, 2, 1):
            s, e = pair_add((s, e), (pltpu.roll(s, step, 0), pltpu.roll(e, step, 0)))
        high = jnp.where(sub == k, s, high)
        low = jnp.where(sub == k, e, low)
    pad = jnp.zeros((LEN - 16, LEN), F32)
    turned = jnp.concatenate([high, low, pad], axis=0).T
    s, e = column_sums(turned)
    return s + pltpu.roll(e, 16, 1)


def column_sums(x):
    parts = [(x[8 * i : 8 * i + 8], jnp.zeros((8, LEN), F32)) for i in range(16)]
    while len(parts) > 1:
        parts = [pair_add(parts[i], parts[i + 1]) for i in range(0, len(parts), 2)]
    s, e = parts[0]
    for step in (4, 2, 1):
        s, e = pair_add((s, e), (pltpu.roll(s, step, 0), pltpu.roll(e, step, 0)))
    return s[0:1], e[0:1]


def totals(rows, count):
    s, e = column_sums(rows)
    low = e + pltpu.roll(s, LEN - 8, 1) + pltpu.roll(s, LEN - 16, 1)
    s, low = two_sum(s, low)
    return [(s[0:1, k : k + 1], low[0:1, k : k + 1]) for k in range(count)]


def over_entries(x):
    return scaled(x, 1.0 / ENTRIES)


def place():
    strip, blk = lax.axis_index("strip"), lax.axis_index("blk")
    return strip, blk


def send_halo(payload, vector):
    strip, blk = place()
    for ds, row in ((-1, 0), (1, ROWS - 1)):
        for db in (-1, 0, 1):
            s, j = strip + ds, blk + db
            inside = (s >= 0) & (s < STRIPS) & (j >= 0) & (j < BLKS)

            @pl.when(inside)
            def _():
                payload[s * BLKS + j, 4:8, :] = vector[:, row, :]


def gather_halo(around, vector, left, right, received):
    strip, blk = place()
    for column, own in ((0, left), (1, vector), (2, right)):
        j = blk + column - 1
        column_in = (j >= 0) & (j < BLKS)
        jj = jnp.clip(j, 0, BLKS - 1)
        base = 10 * column
        block = own[...]
        around[:, base + 1 : base + 9, :] = jnp.where(column_in, block, 0.0) if column != 1 else block
        for row, s in ((0, strip - 1), (9, strip + 1)):
            row_in = column_in & (s >= 0) & (s < STRIPS)
            source = jnp.clip(s, 0, STRIPS - 1) * BLKS + jj
            around[:, base + row, :] = jnp.where(row_in, received[source, 4:8, :], 0.0)
    around[:, 30:32, :] = jnp.zeros((4, 2, LEN), F32)


def near(around, near_pair, kernel_hbm, kernels, sems):
    sub = lax.broadcasted_iota(jnp.int32, (8, LEN), 0)

    def chunk(n, total):
        near_copy(kernel_hbm, kernels, sems, n).wait()
        for i in range(NEAR_CHUNK):
            p = n * NEAR_CHUNK + i
            code = near_pair[p]
            t = code // 9
            k = code - 9 * t
            up = k // 3
            source = (k - 3 * up) * 10 + t + up
            for b in range(3):
                row = around[b, pl.ds(source, 1), :]
                left = jnp.where(sub == t, row, 0.0).astype(BF16)
                matrix = kernels[p, :, b].reshape(3 * LEN, LEN)
                total = total + lax.dot_general(left, matrix, TRANS_B, preferred_element_type=F32)
        return total

    return lax.fori_loop(0, NEAR_CHUNKS, chunk, jnp.zeros((8, 3 * LEN), F32))


def near_copy(kernel_hbm, kernels, sems, n):
    part = pl.ds(n * NEAR_CHUNK, NEAR_CHUNK)
    return pltpu.make_async_copy(kernel_hbm.at[part], kernels.at[part], sems.at[n])


def far_copy(hbm, buffer, sems, n):
    part = pl.ds(n * FAR_PER_COPY, FAR_PER_COPY)
    return pltpu.make_async_copy(hbm.at[part], buffer.at[part], sems.at[n])


def split3(x):
    a = x.astype(BF16)
    rest = x - a.astype(F32)
    b = rest.astype(BF16)
    c = (rest - b.astype(F32)).astype(BF16)
    return a, b, c


def far(payload, vector, source_row, right_hbm, left_hbm, right, left, right_sems, left_sems, gathered, parts):
    for d in range(DEVICES):
        gathered[:, d, :] = vector[0:3, source_row[d], :]
    sub = lax.broadcasted_iota(jnp.int32, (FAR_CHUNK, FAR_CHUNK * RANK), 0)
    lane = lax.broadcasted_iota(jnp.int32, (FAR_CHUNK, FAR_CHUNK * RANK), 1)
    own = lane // RANK == sub

    def stacked(x):
        if parts == 1:
            return x.astype(BF16)
        return jnp.concatenate([piece.astype(F32) for piece in split3(x)], axis=0).astype(BF16)

    def summed(x):
        if parts == 1:
            return x
        return x[0:8] + (x[8:16] + x[16:24])

    per_copy = FAR_PER_COPY // FAR_CHUNK

    def chunk(n, carry):
        @pl.when(lax.rem(n, per_copy) == 0)
        def _():
            far_copy(right_hbm, right, right_sems, n // per_copy).wait()
            far_copy(left_hbm, left, left_sems, n // per_copy).wait()

        d = pl.ds(pl.multiple_of(n * FAR_CHUNK, FAR_CHUNK), FAR_CHUNK)
        c = jnp.zeros((8 * parts, FAR_CHUNK * RANK), F32)
        for b in range(3):
            matrix = right[d, b].reshape(FAR_CHUNK * RANK, LEN)
            c = c + lax.dot_general(stacked(gathered[b, d, :]), matrix, TRANS_B, preferred_element_type=F32)
        c = stacked(jnp.where(own, summed(c), 0.0))
        for a in range(3):
            matrix = left[d, a].reshape(FAR_CHUNK * RANK, LEN)
            payload[d, a, :] = summed(lax.dot_general(c, matrix, PLAIN, preferred_element_type=F32))
        return carry

    lax.fori_loop(0, FAR_CHUNKS, chunk, 0, unroll=2)


def far_sum(received, target):
    sub = lax.broadcasted_iota(jnp.int32, (8, LEN), 0).astype(F32)

    def some(n, totals):
        out = list(totals)
        for i in range(8):
            g = n * 8 + i
            hit = target(g) == sub
            for a in range(3):
                k = 3 * (i % 2) + a
                out[k] = out[k] + jnp.where(hit, received[g, a : a + 1, :], 0.0)
        return tuple(out)

    z = lax.fori_loop(0, DEVICES // 8, some, (jnp.zeros((8, LEN), F32),) * 6)
    return [z[a] + z[3 + a] for a in range(3)]


def flux(around, conductivity):
    pressure = around[3, 11:19, :]
    lane = lax.broadcasted_iota(jnp.int32, (8, LEN), 1)
    west = pltpu.roll(jnp.where(lane == LEN - 1, around[3, 1:9, :], pressure), 1, 1)
    east = pltpu.roll(jnp.where(lane == 0, around[3, 21:29, :], pressure), LEN - 1, 1)
    total = conductivity[0] * (around[3, 10:18, :] - pressure) + conductivity[1] * (around[3, 12:20, :] - pressure)
    return total + conductivity[2] * (west - pressure) + conductivity[3] * (east - pressure)


def image_of(vector, near_part, far_part, flux_sum):
    out = [vector[a] + near_part[:, a * LEN : (a + 1) * LEN] + far_part[a] for a in range(3)]
    out[0] = out[0] - vector[3]
    return out + [vector[3] + vector[0] - flux_sum]


def far_scratch():
    return [
        pltpu.VMEM((DEVICES, 3, RANK, LEN), BF16),
        pltpu.VMEM((DEVICES, 3, RANK, LEN), BF16),
        pltpu.SemaphoreType.DMA((FAR_COPIES,)),
        pltpu.SemaphoreType.DMA((FAR_COPIES,)),
        pltpu.VMEM((3, DEVICES, LEN), F32),
    ]


def near_scratch():
    return [
        pltpu.VMEM((PAIRS, 3, 3, LEN, LEN), BF16),
        pltpu.SemaphoreType.DMA((NEAR_CHUNKS,)),
    ]


def start_far(right_hbm, left_hbm, right, left, right_sems, left_sems):
    for n in range(FAR_COPIES):
        far_copy(right_hbm, right, right_sems, n).start()
        far_copy(left_hbm, left, left_sems, n).start()


def start_near(kernel_hbm, kernels, sems):
    for n in range(NEAR_CHUNKS):
        near_copy(kernel_hbm, kernels, sems, n).start()


def first_far(source_row, target_row, vector, right_hbm, left_hbm, payload, right, left, right_sems, left_sems, gathered):
    start_far(right_hbm, left_hbm, right, left, right_sems, left_sems)
    payload[:, 4:8, :] = jnp.zeros((DEVICES, 4, LEN), F32)
    send_halo(payload, vector)
    for d in range(DEVICES):
        payload[d, 3:4, :] = jnp.full((1, LEN), target_row[d], jnp.int32).astype(F32)
    far(payload, vector, source_row, right_hbm, left_hbm, right, left, right_sems, left_sems, gathered, 1)


def middle(
    near_pair, source_row, vector, conductivity, left_side, right_side, received, kernel_hbm, right_hbm, left_hbm,
    image, far_part, around, payload,
    rounded, kernels, near_sems, right, left, right_sems, left_sems, gathered,
):
    start_near(kernel_hbm, kernels, near_sems)
    start_far(right_hbm, left_hbm, right, left, right_sems, left_sems)
    gather_halo(around, vector, left_side, right_side, received)
    rounded[...] = around[0:3].astype(BF16).astype(F32)
    payload[:, 4:8, :] = jnp.zeros((DEVICES, 4, LEN), F32)
    arrived = far_sum(received, lambda g: received[g, 3:4, :])
    for a in range(3):
        far_part[a] = arrived[a]
    flux_sum = flux(around, conductivity)
    near_part = near(rounded, near_pair, kernel_hbm, kernels, near_sems)
    own = [vector[c] for c in range(4)]
    result = image_of(own, near_part, arrived, flux_sum)
    for c in range(4):
        image[c] = result[c]
    send_halo(payload, image)
    row = dot_row([(own, own), (own, result), (result, result)])
    payload[:, 3, :] = jnp.broadcast_to(row, (DEVICES, LEN))
    far(payload, image, source_row, right_hbm, left_hbm, right, left, right_sems, left_sems, gathered, 3)


def last(
    near_pair, vector, image, conductivity, left_side, right_side, target, received, far_one, around_one, kernel_hbm,
    first, image_two, scalars, rows,
    around, rounded, kernels, near_sems,
):
    start_near(kernel_hbm, kernels, near_sems)
    gather_halo(around, image, left_side, right_side, received)
    vv, vi, ii = totals(received[:, 3, :], 3)
    h = over_entries(vi)
    h0 = h[0]
    h0_pair = (h0, jnp.zeros_like(h0))
    square = pair_add(ii, pair_add(scaled(neg(pair_mul(h0_pair, vi)), 2.0), pair_mul(pair_mul(h0_pair, h0_pair), vv)))
    beta1 = jnp.sqrt(jnp.maximum(square[0], 0.0) / ENTRIES + EPSILON)
    h0_wide = jnp.broadcast_to(h0, (8, LEN))
    beta_wide = jnp.broadcast_to(beta1, (8, LEN))
    for c in range(4):
        for r in range(0, HALO, 8):
            around[c, r : r + 8, :] = (around[c, r : r + 8, :] - h0_wide * around_one[c, r : r + 8, :]) / beta_wide
    rounded[...] = around[0:3].astype(BF16).astype(F32)
    own = [around[c, 11:19, :] for c in range(4)]
    for c in range(4):
        first[c] = own[c]
    arrived = far_sum(received, lambda g: target[g, 3:4, :])
    far_part = [(arrived[a] - h0_wide * far_one[a]) / beta_wide for a in range(3)]
    flux_sum = flux(around, conductivity)
    near_part = near(rounded, near_pair, kernel_hbm, kernels, near_sems)
    result = image_of(own, near_part, far_part, flux_sum)
    for c in range(4):
        image_two[c] = result[c]
    start = [vector[c] for c in range(4)]
    row = dot_row([(start, result), (own, result), (result, result), (start, start), (start, own), (own, own)])
    rows[...] = jnp.broadcast_to(row, (DEVICES, LEN))
    lane = lax.broadcasted_iota(jnp.int32, (1, LEN), 1)
    scalars[...] = jnp.where(lane == 0, h0, beta1)


def finish(vector, first, image, scalars, rows, krylov, hessenberg):
    si, fi, ii, ss, sf, ff = totals(rows[...], 6)
    g0, g1 = over_entries(si)[0], over_entries(fi)[0]
    zero = jnp.zeros_like(g0)
    p0, p1 = (g0, zero), (g1, zero)
    square = pair_add(ii, scaled(neg(pair_add(pair_mul(p0, si), pair_mul(p1, fi))), 2.0))
    cross = scaled(pair_mul(pair_mul(p0, p1), sf), 2.0)
    square = pair_add(square, pair_add(cross, pair_add(pair_mul(pair_mul(p0, p0), ss), pair_mul(pair_mul(p1, p1), ff))))
    beta2 = jnp.sqrt(jnp.maximum(square[0], 0.0) / ENTRIES + EPSILON)
    g0_wide, g1_wide, beta_wide = (jnp.broadcast_to(x, (8, LEN)) for x in (g0, g1, beta2))
    for c in range(4):
        krylov[0, c] = first[c]
        krylov[1, c] = (image[c] - g0_wide * vector[c] - g1_wide * first[c]) / beta_wide
    lane = lax.broadcasted_iota(jnp.int32, (1, LEN), 1)
    out = jnp.where(lane < 2, scalars[...], jnp.where(lane == 2, g0, jnp.where(lane == 3, g1, beta2)))
    hessenberg[...] = out


def shape(*dims):
    return jax.ShapeDtypeStruct(dims, F32)


def params(mib):
    return pltpu.CompilerParams(vmem_limit_bytes=mib * 1024 * 1024)


def exchange(x):
    return lax.all_to_all(x, ("strip", "blk"), 0, 0, tiled=True)


def sides(vector):
    up = [(i, (i + 1) % BLKS) for i in range(BLKS)]
    down = [(j, i) for i, j in up]
    return lax.ppermute(vector, "blk", up), lax.ppermute(vector, "blk", down)


def local(vector, conductivity, near_kernel, near_pair, far_right, far_left, far_source_row, far_target_row):
    right = jnp.transpose(far_right[0], (0, 2, 1, 3))
    left = jnp.transpose(far_left[0], (0, 2, 1, 3))
    source_row, target_row = far_source_row[0], far_target_row[0]
    block, halo, slots = shape(4, ROWS, LEN), shape(4, HALO, LEN), shape(DEVICES, 8, LEN)

    left_side, right_side = sides(vector)
    payload = pl.pallas_call(
        first_far,
        out_shape=slots,
        in_specs=[SMEM, SMEM, VMEM, ANY, ANY],
        out_specs=VMEM,
        scratch_shapes=far_scratch(),
        compiler_params=params(24),
        name="first_far",
    )(source_row, target_row, vector, right, left)
    received_one = exchange(payload)
    image, far_part, around, payload = pl.pallas_call(
        middle,
        out_shape=(block, shape(3, ROWS, LEN), halo, slots),
        in_specs=[SMEM, SMEM, VMEM, VMEM, VMEM, VMEM, VMEM, ANY, ANY, ANY],
        out_specs=(VMEM,) * 4,
        scratch_shapes=[pltpu.VMEM((3, HALO, LEN), F32)] + near_scratch() + far_scratch(),
        compiler_params=params(40),
        name="middle",
    )(near_pair, source_row, vector, conductivity, left_side, right_side, received_one, near_kernel, right, left)
    left_side, right_side = sides(image)
    received_two = exchange(payload)
    first, image_two, scalars, rows = pl.pallas_call(
        last,
        out_shape=(block, block, shape(1, LEN), shape(DEVICES, LEN)),
        in_specs=[SMEM] + [VMEM] * 9 + [ANY],
        out_specs=(VMEM,) * 4,
        scratch_shapes=[pltpu.VMEM((4, HALO, LEN), F32), pltpu.VMEM((3, HALO, LEN), F32)] + near_scratch(),
        compiler_params=params(32),
        name="last",
    )(
        near_pair, vector, image, conductivity, left_side, right_side, received_one, received_two, far_part, around,
        near_kernel,
    )
    rows = exchange(rows)
    krylov, hessenberg = pl.pallas_call(
        finish,
        out_shape=(shape(2, 4, ROWS, LEN), shape(1, LEN)),
        in_specs=[VMEM] * 5,
        out_specs=(VMEM, VMEM),
        name="finish",
    )(vector, first, image_two, scalars, rows)
    return krylov, hessenberg[0, 0:5]


def solution(mesh):
    in_specs = (
        P(None, "strip", "blk"),
        P(None, "strip", "blk"),
        P(("strip", "blk"), None, None, None, None),
        P(("strip", "blk")),
        P(("strip", "blk"), None, None, None, None),
        P(("strip", "blk"), None, None, None, None),
        P(("strip", "blk"), None),
        P(("strip", "blk"), None),
    )
    out_specs = (P(None, None, "strip", "blk"), P())
    return jax.shard_map(local, mesh=mesh, in_specs=in_specs, out_specs=out_specs, check_vma=False)
```

```python
import functools

import jax
import jax.numpy as jnp
from jax import lax
from jax.experimental import pallas as pl
from jax.experimental.pallas import tpu as pltpu
from jax.sharding import PartitionSpec as P

EPSILON = 1e-06
STRIPS, BLKS, DEVICES = 8, 16, 128
ROWS, LEN, RANK, PAIRS = 8, 128, 32, 48
ENTRIES = float(4 * STRIPS * ROWS * BLKS * LEN)
HALO = 32
NEAR_CHUNK = 8
NEAR_CHUNKS = PAIRS // NEAR_CHUNK
FAR_CHUNK = 16
FAR_CHUNKS = DEVICES // FAR_CHUNK
FAR_PER_COPY = 2
FAR_COPIES = FAR_CHUNKS // FAR_PER_COPY
BF16, F32 = jnp.bfloat16, jnp.float32
TRANS_B = (((1,), (1,)), ((), ()))
PLAIN = (((1,), (0,)), ((), ()))
VMEM = pl.BlockSpec(memory_space=pltpu.VMEM)
SMEM = pl.BlockSpec(memory_space=pltpu.SMEM)
ANY = pl.BlockSpec(memory_space=pl.ANY)
HBM = pl.BlockSpec(memory_space=pltpu.HBM)


def two_sum(a, b):
    s = a + b
    t = s - a
    return s, (a - (s - t)) + (b - t)


def halves(a):
    c = a * 4097.0
    hi = c - (c - a)
    return hi, a - hi


def two_prod(a, b):
    p = a * b
    ah, al = halves(a)
    bh, bl = halves(b)
    return p, ((ah * bh - p) + ah * bl + al * bh) + al * bl


def pair_add(x, y):
    s, e = two_sum(x[0], y[0])
    return two_sum(s, e + (x[1] + y[1]))


def pair_mul(x, y):
    p, e = two_prod(x[0], y[0])
    return two_sum(p, e + (x[0] * y[1] + x[1] * y[0]))


def neg(x):
    return -x[0], -x[1]


def scaled(x, power_of_two):
    return x[0] * power_of_two, x[1] * power_of_two


def dot_row(pairs):
    sub = lax.broadcasted_iota(jnp.int32, (8, LEN), 0)
    high = jnp.zeros((8, LEN), F32)
    low = jnp.zeros((8, LEN), F32)
    for k, (a, b) in enumerate(pairs):
        s, e = two_prod(a[0], b[0])
        for c in range(1, 4):
            s, e = pair_add((s, e), two_prod(a[c], b[c]))
        for step in (4, 2, 1):
            s, e = pair_add((s, e), (pltpu.roll(s, step, 0), pltpu.roll(e, step, 0)))
        high = jnp.where(sub == k, s, high)
        low = jnp.where(sub == k, e, low)
    pad = jnp.zeros((LEN - 16, LEN), F32)
    turned = jnp.concatenate([high, low, pad], axis=0).T
    s, e = column_sums(turned)
    return s + pltpu.roll(e, 16, 1)


def column_sums(x):
    parts = [(x[8 * i : 8 * i + 8], jnp.zeros((8, LEN), F32)) for i in range(16)]
    while len(parts) > 1:
        parts = [pair_add(parts[i], parts[i + 1]) for i in range(0, len(parts), 2)]
    s, e = parts[0]
    for step in (4, 2, 1):
        s, e = pair_add((s, e), (pltpu.roll(s, step, 0), pltpu.roll(e, step, 0)))
    return s[0:1], e[0:1]


def totals(rows, count):
    s, e = column_sums(rows)
    low = e + pltpu.roll(s, LEN - 8, 1) + pltpu.roll(s, LEN - 16, 1)
    s, low = two_sum(s, low)
    return [(s[0:1, k : k + 1], low[0:1, k : k + 1]) for k in range(count)]


def over_entries(x):
    return scaled(x, 1.0 / ENTRIES)


def place():
    strip, blk = lax.axis_index("strip"), lax.axis_index("blk")
    return strip, blk


def near(around, near_pair, kernel_hbm, kernels, sems):
    sub = lax.broadcasted_iota(jnp.int32, (8, LEN), 0)

    def chunk(n, total):
        near_copy(kernel_hbm, kernels, sems, n).wait()
        rows, matrices = [], []
        for i in range(NEAR_CHUNK):
            p = n * NEAR_CHUNK + i
            code = near_pair[p]
            t = code // 9
            k = code - 9 * t
            up = k // 3
            source = (k - 3 * up) * 10 + t + up
            for b in range(3):
                rows.append(jnp.where(sub == t, around[b, pl.ds(source, 1), :], 0.0))
                matrices.append(kernels[p, :, b].reshape(3 * LEN, LEN))
        left = jnp.concatenate(split3(jnp.concatenate(rows, axis=1)), axis=0)
        matrix = jnp.concatenate(matrices, axis=1)
        return total + lax.dot_general(left, matrix, TRANS_B, preferred_element_type=F32)

    total = lax.fori_loop(0, NEAR_CHUNKS, chunk, jnp.zeros((24, 3 * LEN), F32))
    return total[0:8], total[0:8] + (total[8:16] + total[16:24])


def near_copy(kernel_hbm, kernels, sems, n):
    part = pl.ds(n * NEAR_CHUNK, NEAR_CHUNK)
    return pltpu.make_async_copy(kernel_hbm.at[part], kernels.at[part], sems.at[n])


def far_copy(hbm, buffer, sems, n):
    part = pl.ds(n * FAR_CHUNK * FAR_PER_COPY, FAR_CHUNK * FAR_PER_COPY)
    return pltpu.make_async_copy(hbm.at[part], buffer.at[part], sems.at[n])


def split3(x):
    a = x.astype(BF16)
    rest = x - a.astype(F32)
    b = rest.astype(BF16)
    c = (rest - b.astype(F32)).astype(BF16)
    return a, b, c


def far(payload, vector, source_row, right_hbm, left_hbm, right, left, right_sems, left_sems, gathered, coefficients, parts):
    row = lax.broadcasted_iota(jnp.int32, (LEN, LEN), 0)
    from_row = jnp.where(row == source_row, 1.0, 0.0).T.astype(BF16)
    pieces = [[x.astype(BF16)] if parts == 1 else split3(x) for x in (vector[b] for b in range(3))]
    below = jnp.zeros((LEN - ROWS, LEN), F32)
    sources = [jnp.concatenate([pieces[b][k].astype(F32), below], axis=0).astype(BF16) for k in range(parts) for b in range(3)]
    sources = jnp.concatenate(sources, axis=1)
    gathered[...] = lax.dot_general(from_row, sources, PLAIN, preferred_element_type=F32).astype(BF16)
    rows = FAR_CHUNK * RANK
    sub = lax.broadcasted_iota(jnp.int32, (FAR_CHUNK, rows), 0)
    lane = lax.broadcasted_iota(jnp.int32, (FAR_CHUNK, rows), 1)
    own = lane // RANK == sub

    def summed(x):
        if parts == 1:
            return x
        return x[0:FAR_CHUNK] + (x[FAR_CHUNK : 2 * FAR_CHUNK] + x[2 * FAR_CHUNK :])

    for n in range(FAR_CHUNKS):
        if n % FAR_PER_COPY == 0:
            far_copy(right_hbm, right, right_sems, n // FAR_PER_COPY).wait()
        d = pl.ds(n * FAR_CHUNK, FAR_CHUNK)
        source = jnp.concatenate([gathered[d, 3 * LEN * k : 3 * LEN * (k + 1)] for k in range(parts)], axis=0)
        matrix = jnp.concatenate([right[d, b].reshape(rows, LEN) for b in range(3)], axis=1)
        c = summed(lax.dot_general(source, matrix, TRANS_B, preferred_element_type=F32))
        c = jnp.where(own, c, 0.0)
        coefficients[n] = c.astype(BF16) if parts == 1 else jnp.concatenate(split3(c), axis=0)
    for n in range(FAR_CHUNKS):
        if n % FAR_PER_COPY == 0:
            far_copy(left_hbm, left, left_sems, n // FAR_PER_COPY).wait()
        d = pl.ds(n * FAR_CHUNK, FAR_CHUNK)
        matrix = jnp.concatenate([left[d, a].reshape(rows, LEN) for a in range(3)], axis=1)
        result = summed(lax.dot_general(coefficients[n], matrix, PLAIN, preferred_element_type=F32))
        for a in range(3):
            payload[d, a, :] = result[:, a * LEN : (a + 1) * LEN]


def far_sum(received, target):
    sub = lax.broadcasted_iota(jnp.int32, (8, LEN), 0).astype(F32)

    def some(n, totals):
        out = list(totals)
        for i in range(8):
            g = n * 8 + i
            hit = target(g) == sub
            for a in range(3):
                k = 3 * (i % 2) + a
                out[k] = out[k] + jnp.where(hit, received[g, a : a + 1, :], 0.0)
        return tuple(out)

    z = lax.fori_loop(0, DEVICES // 8, some, (jnp.zeros((8, LEN), F32),) * 6)
    return [z[a] + z[3 + a] for a in range(3)]


def flux(around, conductivity):
    pressure = around[3, 11:19, :]
    lane = lax.broadcasted_iota(jnp.int32, (8, LEN), 1)
    west = pltpu.roll(jnp.where(lane == LEN - 1, around[3, 1:9, :], pressure), 1, 1)
    east = pltpu.roll(jnp.where(lane == 0, around[3, 21:29, :], pressure), LEN - 1, 1)
    total = conductivity[0] * (around[3, 10:18, :] - pressure) + conductivity[1] * (around[3, 12:20, :] - pressure)
    return total + conductivity[2] * (west - pressure) + conductivity[3] * (east - pressure)


def image_of(vector, local, far_part):
    out = [vector[a] + local[a] + far_part[a] for a in range(3)]
    out[0] = out[0] - vector[3]
    return out + [vector[3] + vector[0] - local[3]]


def far_scratch(parts, rows):
    return [
        pltpu.VMEM((DEVICES, 3, RANK, LEN), BF16),
        pltpu.VMEM((DEVICES, 3, RANK, LEN), BF16),
        pltpu.SemaphoreType.DMA((FAR_COPIES,)),
        pltpu.SemaphoreType.DMA((FAR_COPIES,)),
        pltpu.VMEM((DEVICES, parts * 3 * LEN), BF16),
        pltpu.VMEM((FAR_CHUNKS, parts * FAR_CHUNK, FAR_CHUNK * RANK), BF16),
        pltpu.VMEM((rows, 1, LEN), jnp.int32),
        pltpu.SemaphoreType.DMA((rows,)),
    ]


def near_scratch():
    return [
        pltpu.VMEM((PAIRS, 3, 3, LEN, LEN), BF16),
        pltpu.SemaphoreType.DMA((NEAR_CHUNKS,)),
    ]


def start_far(right_hbm, left_hbm, right, left, right_sems, left_sems):
    for n in range(FAR_COPIES):
        far_copy(right_hbm, right, right_sems, n).start()
    for n in range(FAR_COPIES):
        far_copy(left_hbm, left, left_sems, n).start()


def row_copies(sources, rows, sems):
    return [pltpu.make_async_copy(source, rows.at[i], sems.at[i]) for i, source in enumerate(sources)]


def start_near(kernel_hbm, kernels, sems):
    for n in range(NEAR_CHUNKS):
        near_copy(kernel_hbm, kernels, sems, n).start()


def first_far(
    source_hbm, target_hbm, vector, after_0, after_1, right_hbm, left_hbm, payload,
    right, left, right_sems, left_sems, gathered, coefficients, rows, row_sems,
):
    copies = row_copies((source_hbm, target_hbm), rows, row_sems)
    for copy in copies:
        copy.start()
    start_far(right_hbm, left_hbm, right, left, right_sems, left_sems)
    for copy in copies:
        copy.wait()
    payload[:, 3, :] = jnp.broadcast_to(rows[1].astype(F32), (DEVICES, LEN)).T
    far(payload, vector, rows[0], right_hbm, left_hbm, right, left, right_sems, left_sems, gathered, coefficients, 1)


def second_far(
    source_hbm, vector, row, after_0, after_1, right_hbm, left_hbm, payload,
    right, left, right_sems, left_sems, gathered, coefficients, rows, row_sems,
):
    (copy,) = row_copies((source_hbm,), rows, row_sems)
    copy.start()
    start_far(right_hbm, left_hbm, right, left, right_sems, left_sems)
    payload[:, 3, :] = jnp.broadcast_to(row[...], (DEVICES, LEN))
    copy.wait()
    far(payload, vector, rows[0], right_hbm, left_hbm, right, left, right_sems, left_sems, gathered, coefficients, 3)


def edges(vector, swap_a, swap_b, out):
    strip, _ = place()
    even = lax.rem(strip, 2) == 0
    above = jnp.where(even, swap_b[:, ROWS - 1, :], swap_a[:, ROWS - 1, :])
    below = jnp.where(even, swap_a[:, 0, :], swap_b[:, 0, :])
    out[0:4] = vector[...]
    out[4, 0:4, :] = jnp.where(strip > 0, above, 0.0)
    out[4, 4:8, :] = jnp.where(strip < STRIPS - 1, below, 0.0)


def local_part(near_pair, conductivity, own, left, right, kernel_hbm, rounded, full, around, kernels, sems):
    start_near(kernel_hbm, kernels, sems)
    _, blk = place()
    for column, blocks, inside in ((0, left, blk > 0), (1, own, None), (2, right, blk < BLKS - 1)):
        keep = (lambda x: x) if inside is None else (lambda x, inside=inside: jnp.where(inside, x, 0.0))
        base = 10 * column
        around[:, base + 1 : base + 9, :] = keep(blocks[0:4])
        around[:, base, :] = keep(blocks[4, 0:4, :])
        around[:, base + 9, :] = keep(blocks[4, 4:8, :])
    flux_sum = flux(around, conductivity)
    rounded[3] = flux_sum
    full[3] = flux_sum
    near_rounded, near_full = near(around, near_pair, kernel_hbm, kernels, sems)
    for a in range(3):
        rounded[a] = near_rounded[:, a * LEN : (a + 1) * LEN]
        full[a] = near_full[:, a * LEN : (a + 1) * LEN]


def first_image(vector, local, received, image, far_part, row):
    arrived = far_sum(received, lambda g: received[g, 3:4, :])
    for a in range(3):
        far_part[a] = arrived[a]
    own = [vector[c] for c in range(4)]
    result = image_of(own, local, arrived)
    for c in range(4):
        image[c] = result[c]
    row[...] = dot_row([(own, own), (own, result), (result, result)])


def second_image(vector, image, local_one, local_two, target, received, far_one, first, image_two, scalars, rows):
    vv, vi, ii = totals(received[:, 3, :], 3)
    h = over_entries(vi)
    h0 = h[0]
    h0_pair = (h0, jnp.zeros_like(h0))
    square = pair_add(ii, pair_add(scaled(neg(pair_mul(h0_pair, vi)), 2.0), pair_mul(pair_mul(h0_pair, h0_pair), vv)))
    beta1 = jnp.sqrt(jnp.maximum(square[0], 0.0) / ENTRIES + EPSILON)
    h0_wide = jnp.broadcast_to(h0, (8, LEN))
    beta_wide = jnp.broadcast_to(beta1, (8, LEN))

    def of_first(of_image, of_vector):
        return (of_image - h0_wide * of_vector) / beta_wide

    start = [vector[c] for c in range(4)]
    own = [of_first(image[c], start[c]) for c in range(4)]
    for c in range(4):
        first[c] = own[c]
    arrived = far_sum(received, lambda g: target[g, 3:4, :])
    far_part = [of_first(arrived[a], far_one[a]) for a in range(3)]
    local = [of_first(local_two[c], local_one[c]) for c in range(4)]
    result = image_of(own, local, far_part)
    for c in range(4):
        image_two[c] = result[c]
    row = dot_row([(start, result), (own, result), (result, result), (start, start), (start, own), (own, own)])
    rows[...] = jnp.broadcast_to(row, (DEVICES, LEN))
    lane = lax.broadcasted_iota(jnp.int32, (1, LEN), 1)
    scalars[...] = jnp.where(lane == 0, h0, beta1)


def finish(vector, first, image, scalars, rows, krylov, hessenberg):
    si, fi, ii, ss, sf, ff = totals(rows[...], 6)
    g0, g1 = over_entries(si)[0], over_entries(fi)[0]
    zero = jnp.zeros_like(g0)
    p0, p1 = (g0, zero), (g1, zero)
    square = pair_add(ii, scaled(neg(pair_add(pair_mul(p0, si), pair_mul(p1, fi))), 2.0))
    cross = scaled(pair_mul(pair_mul(p0, p1), sf), 2.0)
    square = pair_add(square, pair_add(cross, pair_add(pair_mul(pair_mul(p0, p0), ss), pair_mul(pair_mul(p1, p1), ff))))
    beta2 = jnp.sqrt(jnp.maximum(square[0], 0.0) / ENTRIES + EPSILON)
    g0_wide, g1_wide, beta_wide = (jnp.broadcast_to(x, (8, LEN)) for x in (g0, g1, beta2))
    for c in range(4):
        krylov[0, c] = first[c]
        krylov[1, c] = (image[c] - g0_wide * vector[c] - g1_wide * first[c]) / beta_wide
    for i, value in enumerate((scalars[0, 0], scalars[0, 1], g0[0, 0], g1[0, 0], beta2[0, 0])):
        hessenberg[i] = value


def shape(*dims):
    return jax.ShapeDtypeStruct(dims, F32)


def limit(mib):
    return pltpu.CompilerParams(vmem_limit_bytes=mib * 1024 * 1024)


def in_hbm(x):
    return pltpu.with_memory_space_constraint(x, pltpu.HBM)


def exchange(x):
    return lax.all_to_all(x, ("strip", "blk"), 0, 0, tiled=True)


def swaps(x, axis, size):
    even = [(i, i ^ 1) for i in range(size)]
    odd = [(i, (i + 1) % size if i % 2 else (i - 1) % size) for i in range(size)]
    return lax.ppermute(x, axis, even), lax.ppermute(x, axis, odd)


def sides(x):
    up = [(i, (i + 1) % BLKS) for i in range(BLKS)]
    down = [(j, i) for i, j in up]
    return lax.ppermute(x, "blk", up), lax.ppermute(x, "blk", down)


def with_halo(vector):
    swap_a, swap_b = swaps(vector, "strip", STRIPS)
    own = pl.pallas_call(edges, out_shape=shape(5, ROWS, LEN), in_specs=[VMEM] * 3, out_specs=VMEM, compiler_params=limit(4), name="edges")(
        vector, swap_a, swap_b
    )
    return (own, *sides(own))


def local(vector, conductivity, near_kernel, near_pair, far_right, far_left, far_source_row, far_target_row):
    right = in_hbm(jnp.transpose(far_right[0], (0, 2, 1, 3)))
    left = in_hbm(jnp.transpose(far_left[0], (0, 2, 1, 3)))
    near_kernel = in_hbm(near_kernel)
    source_row, target_row = in_hbm(far_source_row), in_hbm(far_target_row)
    block, slots, line = shape(4, ROWS, LEN), shape(DEVICES, 4, LEN), shape(1, LEN)

    local_call = functools.partial(
        pl.pallas_call,
        local_part,
        out_shape=(block, block),
        in_specs=[SMEM, VMEM, VMEM, VMEM, VMEM, HBM],
        out_specs=(VMEM, VMEM),
        scratch_shapes=[pltpu.VMEM((4, HALO, LEN), F32)] + near_scratch(),
        compiler_params=limit(20),
        cost_estimate=pl.CostEstimate(flops=4 * 10**8, bytes_accessed=2 * 10**7, transcendentals=0),
        name="local_part",
    )

    blocks = with_halo(vector)
    start = blocks[0]
    payload = pl.pallas_call(
        first_far,
        out_shape=slots,
        in_specs=[HBM, HBM, VMEM, ANY, ANY, HBM, HBM],
        out_specs=VMEM,
        scratch_shapes=far_scratch(1, 2),
        compiler_params=limit(12),
        name="first_far",
    )(source_row, target_row, blocks[0], blocks[1], blocks[2], right, left)
    received_one = exchange(payload)
    rounded_one, local_one = local_call()(near_pair, conductivity, *blocks, near_kernel)
    image, far_one, row = pl.pallas_call(
        first_image,
        out_shape=(block, shape(3, ROWS, LEN), line),
        in_specs=[VMEM] * 3,
        out_specs=(VMEM,) * 3,
        compiler_params=limit(4),
        name="first_image",
    )(start, rounded_one, received_one)
    blocks = with_halo(image)
    payload = pl.pallas_call(
        second_far,
        out_shape=slots,
        in_specs=[HBM, VMEM, VMEM, ANY, ANY, HBM, HBM],
        out_specs=VMEM,
        scratch_shapes=far_scratch(3, 1),
        compiler_params=limit(12),
        name="second_far",
    )(source_row, image, row, blocks[1], blocks[2], right, left)
    received_two = exchange(payload)
    _, local_two = local_call()(near_pair, conductivity, *blocks, near_kernel)
    first, image_two, scalars, rows = pl.pallas_call(
        second_image,
        out_shape=(block, block, line, shape(DEVICES, LEN)),
        in_specs=[VMEM] * 7,
        out_specs=(VMEM,) * 4,
        compiler_params=limit(4),
        name="second_image",
    )(start, image, local_one, local_two, received_one, received_two, far_one)
    rows = exchange(rows)
    krylov, hessenberg = pl.pallas_call(
        finish,
        out_shape=(shape(2, 4, ROWS, LEN), shape(5)),
        in_specs=[VMEM] * 5,
        out_specs=(VMEM, SMEM),
        compiler_params=limit(4),
        name="finish",
    )(start, first, image_two, scalars, rows)
    return krylov, hessenberg


def solution(mesh):
    in_specs = (
        P(None, "strip", "blk"),
        P(None, "strip", "blk"),
        P(("strip", "blk"), None, None, None, None),
        P(("strip", "blk")),
        P(("strip", "blk"), None, None, None, None),
        P(("strip", "blk"), None, None, None, None),
        P(("strip", "blk"), None),
        P(("strip", "blk"), None),
    )
    out_specs = (P(None, None, "strip", "blk"), P())
    return jax.shard_map(local, mesh=mesh, in_specs=in_specs, out_specs=out_specs, check_vma=False)
```

```python
import functools

import jax
import jax.numpy as jnp
from jax import lax
from jax.experimental import pallas as pl
from jax.experimental.pallas import tpu as pltpu
from jax.sharding import PartitionSpec as P

EPSILON = 1e-06
STRIPS, BLKS, DEVICES = 8, 16, 128
ROWS, LEN, RANK, PAIRS = 8, 128, 32, 48
ENTRIES = float(4 * STRIPS * ROWS * BLKS * LEN)
HALO = 32
NEAR_CHUNK = 8
NEAR_CHUNKS = PAIRS // NEAR_CHUNK
FAR_CHUNK = 16
FAR_CHUNKS = DEVICES // FAR_CHUNK
FAR_PER_COPY = 2
FAR_COPIES = FAR_CHUNKS // FAR_PER_COPY
BF16, F32 = jnp.bfloat16, jnp.float32
TRANS_B = (((1,), (1,)), ((), ()))
PLAIN = (((1,), (0,)), ((), ()))
VMEM = pl.BlockSpec(memory_space=pltpu.VMEM)
SMEM = pl.BlockSpec(memory_space=pltpu.SMEM)
ANY = pl.BlockSpec(memory_space=pl.ANY)
HBM = pl.BlockSpec(memory_space=pltpu.HBM)


def two_sum(a, b):
    s = a + b
    t = s - a
    return s, (a - (s - t)) + (b - t)


def halves(a):
    c = a * 4097.0
    hi = c - (c - a)
    return hi, a - hi


def two_prod(a, b):
    p = a * b
    ah, al = halves(a)
    bh, bl = halves(b)
    return p, ((ah * bh - p) + ah * bl + al * bh) + al * bl


def pair_add(x, y):
    s, e = two_sum(x[0], y[0])
    return two_sum(s, e + (x[1] + y[1]))


def pair_mul(x, y):
    p, e = two_prod(x[0], y[0])
    return two_sum(p, e + (x[0] * y[1] + x[1] * y[0]))


def neg(x):
    return -x[0], -x[1]


def scaled(x, power_of_two):
    return x[0] * power_of_two, x[1] * power_of_two


def dot_row(pairs):
    sub = lax.broadcasted_iota(jnp.int32, (8, LEN), 0)
    high = jnp.zeros((8, LEN), F32)
    low = jnp.zeros((8, LEN), F32)
    for k, (a, b) in enumerate(pairs):
        s, e = two_prod(a[0], b[0])
        for c in range(1, 4):
            s, e = pair_add((s, e), two_prod(a[c], b[c]))
        for step in (4, 2, 1):
            s, e = pair_add((s, e), (pltpu.roll(s, step, 0), pltpu.roll(e, step, 0)))
        high = jnp.where(sub == k, s, high)
        low = jnp.where(sub == k, e, low)
    pad = jnp.zeros((LEN - 16, LEN), F32)
    turned = jnp.concatenate([high, low, pad], axis=0).T
    s, e = column_sums(turned)
    return s + pltpu.roll(e, 16, 1)


def column_sums(x):
    parts = [(x[8 * i : 8 * i + 8], jnp.zeros((8, LEN), F32)) for i in range(16)]
    while len(parts) > 1:
        parts = [pair_add(parts[i], parts[i + 1]) for i in range(0, len(parts), 2)]
    s, e = parts[0]
    for step in (4, 2, 1):
        s, e = pair_add((s, e), (pltpu.roll(s, step, 0), pltpu.roll(e, step, 0)))
    return s[0:1], e[0:1]


def totals(rows, count):
    s, e = column_sums(rows)
    low = e + pltpu.roll(s, LEN - 8, 1) + pltpu.roll(s, LEN - 16, 1)
    s, low = two_sum(s, low)
    return [(s[0:1, k : k + 1], low[0:1, k : k + 1]) for k in range(count)]


def over_entries(x):
    return scaled(x, 1.0 / ENTRIES)


def place():
    strip, blk = lax.axis_index("strip"), lax.axis_index("blk")
    return strip, blk


def near(around, near_pair, kernel_hbm, kernels, sems):
    sub = lax.broadcasted_iota(jnp.int32, (8, LEN), 0)

    def chunk(n, total):
        near_copy(kernel_hbm, kernels, sems, n).wait()
        rows, matrices = [], []
        for i in range(NEAR_CHUNK):
            p = n * NEAR_CHUNK + i
            code = near_pair[p]
            t = code // 9
            k = code - 9 * t
            up = k // 3
            source = (k - 3 * up) * 10 + t + up
            for b in range(3):
                rows.append(jnp.where(sub == t, around[b, pl.ds(source, 1), :], 0.0))
                matrices.append(kernels[p, :, b].reshape(3 * LEN, LEN))
        left = jnp.concatenate(split3(jnp.concatenate(rows, axis=1)), axis=0)
        matrix = jnp.concatenate(matrices, axis=1)
        return total + lax.dot_general(left, matrix, TRANS_B, preferred_element_type=F32)

    total = lax.fori_loop(0, NEAR_CHUNKS, chunk, jnp.zeros((24, 3 * LEN), F32))
    return total[0:8], total[0:8] + (total[8:16] + total[16:24])


def near_copy(kernel_hbm, kernels, sems, n):
    part = pl.ds(n * NEAR_CHUNK, NEAR_CHUNK)
    return pltpu.make_async_copy(kernel_hbm.at[part], kernels.at[part], sems.at[n])


def far_copy(hbm, buffer, sems, n):
    part = pl.ds(n * FAR_CHUNK * FAR_PER_COPY, FAR_CHUNK * FAR_PER_COPY)
    return pltpu.make_async_copy(hbm.at[part], buffer.at[part], sems.at[n])


def split3(x):
    a = x.astype(BF16)
    rest = x - a.astype(F32)
    b = rest.astype(BF16)
    c = (rest - b.astype(F32)).astype(BF16)
    return a, b, c


def own_block():
    sub = lax.broadcasted_iota(jnp.int32, (FAR_CHUNK, FAR_CHUNK * RANK), 0)
    lane = lax.broadcasted_iota(jnp.int32, (FAR_CHUNK, FAR_CHUNK * RANK), 1)
    return lane // RANK == sub


def summed(x, parts):
    if parts == 1:
        return x
    return x[0:FAR_CHUNK] + (x[FAR_CHUNK : 2 * FAR_CHUNK] + x[2 * FAR_CHUNK :])


def project(parts, source_hbm, vector_in, right_hbm, coefficients, vector, right, sems, gathered, rows, row_sem, vector_sem):
    copy = pltpu.make_async_copy(source_hbm, rows, row_sem)
    vector_copy = pltpu.make_async_copy(vector_in, vector, vector_sem)
    copy.start()
    vector_copy.start()
    for n in range(FAR_COPIES):
        far_copy(right_hbm, right, sems, n).start()
    vector_copy.wait()
    pieces = [[x.astype(BF16)] if parts == 1 else split3(x) for x in (vector[b] for b in range(3))]
    below = jnp.zeros((LEN - ROWS, LEN), F32)
    sources = [jnp.concatenate([pieces[b][k].astype(F32), below], axis=0).astype(BF16) for k in range(parts) for b in range(3)]
    sources = jnp.concatenate(sources, axis=1)
    row = lax.broadcasted_iota(jnp.int32, (LEN, LEN), 0)
    copy.wait()
    from_row = jnp.where(row == rows[...], 1.0, 0.0).T.astype(BF16)
    gathered[...] = lax.dot_general(from_row, sources, PLAIN, preferred_element_type=F32).astype(BF16)
    own = own_block()
    for n in range(FAR_CHUNKS):
        if n % FAR_PER_COPY == 0:
            far_copy(right_hbm, right, sems, n // FAR_PER_COPY).wait()
        d = pl.ds(n * FAR_CHUNK, FAR_CHUNK)
        source = jnp.concatenate([gathered[d, 3 * LEN * k : 3 * LEN * (k + 1)] for k in range(parts)], axis=0)
        matrix = jnp.concatenate([right[d, b].reshape(FAR_CHUNK * RANK, LEN) for b in range(3)], axis=1)
        c = summed(lax.dot_general(source, matrix, TRANS_B, preferred_element_type=F32), parts)
        c = jnp.where(own, c, 0.0)
        coefficients[n] = c.astype(BF16) if parts == 1 else jnp.concatenate(split3(c), axis=0)


def expand(parts, coefficients, left_hbm, payload, left, sems):
    for n in range(FAR_CHUNKS):
        if n % FAR_PER_COPY == 0:
            far_copy(left_hbm, left, sems, n // FAR_PER_COPY).wait()
        d = pl.ds(n * FAR_CHUNK, FAR_CHUNK)
        matrix = jnp.concatenate([left[d, a].reshape(FAR_CHUNK * RANK, LEN) for a in range(3)], axis=1)
        result = summed(lax.dot_general(coefficients[n], matrix, PLAIN, preferred_element_type=F32), parts)
        for a in range(3):
            payload[d, a, :] = result[:, a * LEN : (a + 1) * LEN]


def far_sum(received, target):
    sub = lax.broadcasted_iota(jnp.int32, (8, LEN), 0).astype(F32)

    def some(n, totals):
        out = list(totals)
        for i in range(8):
            g = n * 8 + i
            hit = target(g) == sub
            for a in range(3):
                k = 3 * (i % 2) + a
                out[k] = out[k] + jnp.where(hit, received[g, a : a + 1, :], 0.0)
        return tuple(out)

    z = lax.fori_loop(0, DEVICES // 8, some, (jnp.zeros((8, LEN), F32),) * 6)
    return [z[a] + z[3 + a] for a in range(3)]


def flux(around, conductivity):
    pressure = around[3, 11:19, :]
    lane = lax.broadcasted_iota(jnp.int32, (8, LEN), 1)
    west = pltpu.roll(jnp.where(lane == LEN - 1, around[3, 1:9, :], pressure), 1, 1)
    east = pltpu.roll(jnp.where(lane == 0, around[3, 21:29, :], pressure), LEN - 1, 1)
    total = conductivity[0] * (around[3, 10:18, :] - pressure) + conductivity[1] * (around[3, 12:20, :] - pressure)
    return total + conductivity[2] * (west - pressure) + conductivity[3] * (east - pressure)


def image_of(vector, local, far_part):
    out = [vector[a] + local[a] + far_part[a] for a in range(3)]
    out[0] = out[0] - vector[3]
    return out + [vector[3] + vector[0] - local[3]]


def far_scratch():
    return [pltpu.VMEM((DEVICES, 3, RANK, LEN), BF16), pltpu.SemaphoreType.DMA((FAR_COPIES,))]


def near_scratch():
    return [
        pltpu.VMEM((PAIRS, 3, 3, LEN, LEN), BF16),
        pltpu.SemaphoreType.DMA((NEAR_CHUNKS,)),
    ]


def start_near(kernel_hbm, kernels, sems):
    for n in range(NEAR_CHUNKS):
        near_copy(kernel_hbm, kernels, sems, n).start()


def first_expand(target_hbm, after, coefficients, left_hbm, payload, left, sems, rows, row_sem):
    copy = pltpu.make_async_copy(target_hbm, rows, row_sem)
    copy.start()
    for n in range(FAR_COPIES):
        far_copy(left_hbm, left, sems, n).start()
    copy.wait()
    payload[:, 3, :] = jnp.broadcast_to(rows[...].astype(F32), (DEVICES, LEN)).T
    expand(1, coefficients, left_hbm, payload, left, sems)


def second_expand(row, after, coefficients, left_hbm, payload, left, sems):
    for n in range(FAR_COPIES):
        far_copy(left_hbm, left, sems, n).start()
    payload[:, 3, :] = jnp.broadcast_to(row[...], (DEVICES, LEN))
    expand(3, coefficients, left_hbm, payload, left, sems)


def edges(vector, swap_a, swap_b, out):
    strip, _ = place()
    even = lax.rem(strip, 2) == 0
    above = jnp.where(even, swap_b[:, ROWS - 1, :], swap_a[:, ROWS - 1, :])
    below = jnp.where(even, swap_a[:, 0, :], swap_b[:, 0, :])
    out[0:4] = vector[...]
    out[4, 0:4, :] = jnp.where(strip > 0, above, 0.0)
    out[4, 4:8, :] = jnp.where(strip < STRIPS - 1, below, 0.0)


def local_part(near_pair, conductivity, own, swap_a, swap_b, kernel_hbm, rounded, full, around, kernels, sems):
    start_near(kernel_hbm, kernels, sems)
    _, blk = place()
    even = lax.rem(blk, 2) == 0
    left = jnp.where(blk > 0, jnp.where(even, swap_b[...], swap_a[...]), 0.0)
    right = jnp.where(blk < BLKS - 1, jnp.where(even, swap_a[...], swap_b[...]), 0.0)
    for column, blocks in enumerate((left, own[...], right)):
        base = 10 * column
        around[:, base + 1 : base + 9, :] = blocks[0:4]
        around[:, base, :] = blocks[4, 0:4]
        around[:, base + 9, :] = blocks[4, 4:8]
    flux_sum = flux(around, conductivity)
    rounded[3] = flux_sum
    full[3] = flux_sum
    near_rounded, near_full = near(around, near_pair, kernel_hbm, kernels, sems)
    for a in range(3):
        rounded[a] = near_rounded[:, a * LEN : (a + 1) * LEN]
        full[a] = near_full[:, a * LEN : (a + 1) * LEN]


def first_image(vector, local, received, image, far_part, row):
    arrived = far_sum(received, lambda g: received[g, 3:4, :])
    for a in range(3):
        far_part[a] = arrived[a]
    own = [vector[c] for c in range(4)]
    result = image_of(own, local, arrived)
    for c in range(4):
        image[c] = result[c]
    row[...] = dot_row([(own, own), (own, result), (result, result)])


def second_image(vector, image, local_one, local_two, target, received, far_one, first, image_two, scalars, rows):
    vv, vi, ii = totals(received[:, 3, :], 3)
    h = over_entries(vi)
    h0 = h[0]
    h0_pair = (h0, jnp.zeros_like(h0))
    square = pair_add(ii, pair_add(scaled(neg(pair_mul(h0_pair, vi)), 2.0), pair_mul(pair_mul(h0_pair, h0_pair), vv)))
    beta1 = jnp.sqrt(jnp.maximum(square[0], 0.0) / ENTRIES + EPSILON)
    h0_wide = jnp.broadcast_to(h0, (8, LEN))
    beta_wide = jnp.broadcast_to(beta1, (8, LEN))

    def of_first(of_image, of_vector):
        return (of_image - h0_wide * of_vector) / beta_wide

    start = [vector[c] for c in range(4)]
    own = [of_first(image[c], start[c]) for c in range(4)]
    for c in range(4):
        first[c] = own[c]
    arrived = far_sum(received, lambda g: target[g, 3:4, :])
    far_part = [of_first(arrived[a], far_one[a]) for a in range(3)]
    local = [of_first(local_two[c], local_one[c]) for c in range(4)]
    result = image_of(own, local, far_part)
    for c in range(4):
        image_two[c] = result[c]
    row = dot_row([(start, result), (own, result), (result, result), (start, start), (start, own), (own, own)])
    rows[...] = jnp.broadcast_to(row, (DEVICES, LEN))
    lane = lax.broadcasted_iota(jnp.int32, (1, LEN), 1)
    scalars[...] = jnp.where(lane == 0, h0, beta1)


def finish(vector, first, image, scalars, rows, krylov, hessenberg):
    si, fi, ii, ss, sf, ff = totals(rows[...], 6)
    g0, g1 = over_entries(si)[0], over_entries(fi)[0]
    zero = jnp.zeros_like(g0)
    p0, p1 = (g0, zero), (g1, zero)
    square = pair_add(ii, scaled(neg(pair_add(pair_mul(p0, si), pair_mul(p1, fi))), 2.0))
    cross = scaled(pair_mul(pair_mul(p0, p1), sf), 2.0)
    square = pair_add(square, pair_add(cross, pair_add(pair_mul(pair_mul(p0, p0), ss), pair_mul(pair_mul(p1, p1), ff))))
    beta2 = jnp.sqrt(jnp.maximum(square[0], 0.0) / ENTRIES + EPSILON)
    g0_wide, g1_wide, beta_wide = (jnp.broadcast_to(x, (8, LEN)) for x in (g0, g1, beta2))
    for c in range(4):
        krylov[0, c] = first[c]
        krylov[1, c] = (image[c] - g0_wide * vector[c] - g1_wide * first[c]) / beta_wide
    for i, value in enumerate((scalars[0, 0], scalars[0, 1], g0[0, 0], g1[0, 0], beta2[0, 0])):
        hessenberg[i] = value


def shape(*dims):
    return jax.ShapeDtypeStruct(dims, F32)


def limit(mib):
    return pltpu.CompilerParams(vmem_limit_bytes=mib * 1024 * 1024)


def in_hbm(x):
    return pltpu.with_memory_space_constraint(x, pltpu.HBM)


def exchange(x):
    return lax.all_to_all(x, ("strip", "blk"), 0, 0, tiled=True)


def swaps(x, axis, size):
    even = [(i, i ^ 1) for i in range(size)]
    odd = [(i, (i + 1) % size if i % 2 else (i - 1) % size) for i in range(size)]
    return lax.ppermute(x, axis, even), lax.ppermute(x, axis, odd)


def own_blocks(parts, source_row, vector, right):
    swap_a, swap_b = swaps(vector, "strip", STRIPS)
    coefficients, vector = projected(parts, source_row, in_hbm(vector) if parts == 1 else vector, right)
    own = pl.pallas_call(
        edges,
        out_shape=shape(5, ROWS, LEN),
        in_specs=[VMEM] * 3,
        out_specs=VMEM,
        compiler_params=limit(4),
        name="edges",
    )(vector, swap_a, swap_b)
    return own, coefficients


def projected(parts, source_row, vector, right):
    return pl.pallas_call(
        functools.partial(project, parts),
        out_shape=(
            jax.ShapeDtypeStruct((FAR_CHUNKS, parts * FAR_CHUNK, FAR_CHUNK * RANK), BF16),
            shape(4, ROWS, LEN),
        ),
        in_specs=[HBM, HBM if parts == 1 else ANY, HBM],
        out_specs=(VMEM, VMEM),
        scratch_shapes=far_scratch()
        + [pltpu.VMEM((DEVICES, parts * 3 * LEN), BF16), pltpu.VMEM((1, LEN), jnp.int32), pltpu.SemaphoreType.DMA, pltpu.SemaphoreType.DMA],
        compiler_params=limit(12),
        cost_estimate=pl.CostEstimate(flops=2 * 10**8, bytes_accessed=10**7, transcendentals=0),
        name="project",
    )(source_row, vector, right)


def local(vector, conductivity, near_kernel, near_pair, far_right, far_left, far_source_row, far_target_row):
    right = in_hbm(jnp.transpose(far_right[0], (0, 2, 1, 3)))
    left = in_hbm(jnp.transpose(far_left[0], (0, 2, 1, 3)))
    near_kernel = in_hbm(near_kernel)
    source_row, target_row = in_hbm(far_source_row), in_hbm(far_target_row)
    block, slots, line = shape(4, ROWS, LEN), shape(DEVICES, 4, LEN), shape(1, LEN)

    local_call = functools.partial(
        pl.pallas_call,
        local_part,
        out_shape=(block, block),
        in_specs=[SMEM, VMEM, VMEM, VMEM, VMEM, HBM],
        out_specs=(VMEM, VMEM),
        scratch_shapes=[pltpu.VMEM((4, HALO, LEN), F32)] + near_scratch(),
        compiler_params=limit(20),
        cost_estimate=pl.CostEstimate(flops=4 * 10**8, bytes_accessed=2 * 10**7, transcendentals=0),
        name="local_part",
    )

    expand_call = functools.partial(
        pl.pallas_call,
        out_shape=slots,
        out_specs=VMEM,
        compiler_params=limit(12),
        cost_estimate=pl.CostEstimate(flops=2 * 10**8, bytes_accessed=10**7, transcendentals=0),
    )

    start, coefficients = own_blocks(1, source_row, vector, right)
    blocks = swaps(start, "blk", BLKS)
    payload = expand_call(
        first_expand,
        in_specs=[HBM, ANY, VMEM, HBM],
        scratch_shapes=far_scratch() + [pltpu.VMEM((1, LEN), jnp.int32), pltpu.SemaphoreType.DMA],
        name="first_expand",
    )(target_row, start, coefficients, left)
    payload, *blocks = lax.optimization_barrier((payload, *blocks))
    blocks = (start, *blocks)
    received_one = exchange(payload)
    rounded_one, local_one = local_call()(near_pair, conductivity, *blocks, near_kernel)
    image, far_one, row = pl.pallas_call(
        first_image,
        out_shape=(block, shape(3, ROWS, LEN), line),
        in_specs=[VMEM] * 3,
        out_specs=(VMEM,) * 3,
        compiler_params=limit(4),
        name="first_image",
    )(start, rounded_one, received_one)
    own, coefficients = own_blocks(3, source_row, image, right)
    blocks = swaps(own, "blk", BLKS)
    payload = expand_call(
        second_expand, in_specs=[VMEM, ANY, VMEM, HBM], scratch_shapes=far_scratch(), name="second_expand"
    )(row, own, coefficients, left)
    payload, *blocks = lax.optimization_barrier((payload, *blocks))
    blocks = (own, *blocks)
    received_two = exchange(payload)
    _, local_two = local_call()(near_pair, conductivity, *blocks, near_kernel)
    first, image_two, scalars, rows = pl.pallas_call(
        second_image,
        out_shape=(block, block, line, shape(DEVICES, LEN)),
        in_specs=[VMEM] * 7,
        out_specs=(VMEM,) * 4,
        compiler_params=limit(4),
        name="second_image",
    )(start, image, local_one, local_two, received_one, received_two, far_one)
    rows = exchange(rows)
    krylov, hessenberg = pl.pallas_call(
        finish,
        out_shape=(shape(2, 4, ROWS, LEN), shape(5)),
        in_specs=[VMEM] * 5,
        out_specs=(VMEM, SMEM),
        compiler_params=limit(4),
        name="finish",
    )(start, first, image_two, scalars, rows)
    return krylov, hessenberg


def solution(mesh):
    in_specs = (
        P(None, "strip", "blk"),
        P(None, "strip", "blk"),
        P(("strip", "blk"), None, None, None, None),
        P(("strip", "blk")),
        P(("strip", "blk"), None, None, None, None),
        P(("strip", "blk"), None, None, None, None),
        P(("strip", "blk"), None),
        P(("strip", "blk"), None),
    )
    out_specs = (P(None, None, "strip", "blk"), P())
    return jax.shard_map(local, mesh=mesh, in_specs=in_specs, out_specs=out_specs, check_vma=False)
```

```python
import functools

import jax
import jax.numpy as jnp
from jax import lax
from jax.experimental import pallas as pl
from jax.experimental.pallas import tpu as pltpu
from jax.sharding import PartitionSpec as P

EPSILON = 1e-06
STRIPS, BLKS, DEVICES = 8, 16, 128
ROWS, LEN, RANK, PAIRS = 8, 128, 32, 48
ENTRIES = float(4 * STRIPS * ROWS * BLKS * LEN)
HALO = 32
NEAR_CHUNK = 8
NEAR_CHUNKS = PAIRS // NEAR_CHUNK
FAR_CHUNK = 16
FAR_CHUNKS = DEVICES // FAR_CHUNK
FAR_PER_COPY = 2
FAR_COPIES = FAR_CHUNKS // FAR_PER_COPY
BF16, F32 = jnp.bfloat16, jnp.float32
TRANS_B = (((1,), (1,)), ((), ()))
PLAIN = (((1,), (0,)), ((), ()))
VMEM = pl.BlockSpec(memory_space=pltpu.VMEM)
SMEM = pl.BlockSpec(memory_space=pltpu.SMEM)
ANY = pl.BlockSpec(memory_space=pl.ANY)
HBM = pl.BlockSpec(memory_space=pltpu.HBM)


def two_sum(a, b):
    s = a + b
    t = s - a
    return s, (a - (s - t)) + (b - t)


def halves(a):
    c = a * 4097.0
    hi = c - (c - a)
    return hi, a - hi


def two_prod(a, b):
    p = a * b
    ah, al = halves(a)
    bh, bl = halves(b)
    return p, ((ah * bh - p) + ah * bl + al * bh) + al * bl


def pair_add(x, y):
    s, e = two_sum(x[0], y[0])
    return two_sum(s, e + (x[1] + y[1]))


def pair_mul(x, y):
    p, e = two_prod(x[0], y[0])
    return two_sum(p, e + (x[0] * y[1] + x[1] * y[0]))


def neg(x):
    return -x[0], -x[1]


def scaled(x, power_of_two):
    return x[0] * power_of_two, x[1] * power_of_two


def dot_row(pairs):
    sub = lax.broadcasted_iota(jnp.int32, (8, LEN), 0)
    high = jnp.zeros((8, LEN), F32)
    low = jnp.zeros((8, LEN), F32)
    for k, (a, b) in enumerate(pairs):
        s, e = two_prod(a[0], b[0])
        for c in range(1, 4):
            s, e = pair_add((s, e), two_prod(a[c], b[c]))
        for step in (4, 2, 1):
            s, e = pair_add((s, e), (pltpu.roll(s, step, 0), pltpu.roll(e, step, 0)))
        high = jnp.where(sub == k, s, high)
        low = jnp.where(sub == k, e, low)
    pad = jnp.zeros((LEN - 16, LEN), F32)
    turned = jnp.concatenate([high, low, pad], axis=0).T
    s, e = column_sums(turned)
    return s + pltpu.roll(e, 16, 1)


def column_sums(x):
    parts = [(x[8 * i : 8 * i + 8], jnp.zeros((8, LEN), F32)) for i in range(16)]
    while len(parts) > 1:
        parts = [pair_add(parts[i], parts[i + 1]) for i in range(0, len(parts), 2)]
    s, e = parts[0]
    for step in (4, 2, 1):
        s, e = pair_add((s, e), (pltpu.roll(s, step, 0), pltpu.roll(e, step, 0)))
    return s[0:1], e[0:1]


def totals(rows, count):
    s, e = column_sums(rows)
    low = e + pltpu.roll(s, LEN - 8, 1) + pltpu.roll(s, LEN - 16, 1)
    s, low = two_sum(s, low)
    return [(s[0:1, k : k + 1], low[0:1, k : k + 1]) for k in range(count)]


def over_entries(x):
    return scaled(x, 1.0 / ENTRIES)


def place():
    strip, blk = lax.axis_index("strip"), lax.axis_index("blk")
    return strip, blk


def near(around, near_pair, kernels, wait):
    sub = lax.broadcasted_iota(jnp.int32, (8, LEN), 0)

    def chunk(n, total):
        wait(n)
        rows, matrices = [], []
        for i in range(NEAR_CHUNK):
            p = n * NEAR_CHUNK + i
            code = near_pair[p]
            t = code // 9
            k = code - 9 * t
            up = k // 3
            source = (k - 3 * up) * 10 + t + up
            for b in range(3):
                rows.append(jnp.where(sub == t, around[b, pl.ds(source, 1), :], 0.0))
                matrices.append(kernels[p, :, b].reshape(3 * LEN, LEN))
        left = jnp.concatenate(split3(jnp.concatenate(rows, axis=1)), axis=0)
        matrix = jnp.concatenate(matrices, axis=1)
        return total + lax.dot_general(left, matrix, TRANS_B, preferred_element_type=F32)

    total = lax.fori_loop(0, NEAR_CHUNKS, chunk, jnp.zeros((24, 3 * LEN), F32))
    return total[0:8], total[0:8] + (total[8:16] + total[16:24])


def near_copy(kernel_hbm, kernels, sems, n):
    part = pl.ds(n * NEAR_CHUNK, NEAR_CHUNK)
    return pltpu.make_async_copy(kernel_hbm.at[part], kernels.at[part], sems.at[n])


def far_copy(hbm, buffer, sems, n):
    part = pl.ds(n * FAR_CHUNK * FAR_PER_COPY, FAR_CHUNK * FAR_PER_COPY)
    return pltpu.make_async_copy(hbm.at[part], buffer.at[part], sems.at[n])


def split3(x):
    a = x.astype(BF16)
    rest = x - a.astype(F32)
    b = rest.astype(BF16)
    c = (rest - b.astype(F32)).astype(BF16)
    return a, b, c


def own_block():
    sub = lax.broadcasted_iota(jnp.int32, (FAR_CHUNK, FAR_CHUNK * RANK), 0)
    lane = lax.broadcasted_iota(jnp.int32, (FAR_CHUNK, FAR_CHUNK * RANK), 1)
    return lane // RANK == sub


def summed(x, parts):
    if parts == 1:
        return x
    return x[0:FAR_CHUNK] + (x[FAR_CHUNK : 2 * FAR_CHUNK] + x[2 * FAR_CHUNK :])


def project(parts, source_row, vector, coefficients, right, gathered, copies):
    pieces = [[x.astype(BF16)] if parts == 1 else split3(x) for x in (vector[b] for b in range(3))]
    below = jnp.zeros((LEN - ROWS, LEN), F32)
    sources = [jnp.concatenate([pieces[b][k].astype(F32), below], axis=0).astype(BF16) for k in range(parts) for b in range(3)]
    sources = jnp.concatenate(sources, axis=1)
    row = lax.broadcasted_iota(jnp.int32, (LEN, LEN), 0)
    from_row = jnp.where(row == source_row, 1.0, 0.0).T.astype(BF16)
    gathered[...] = lax.dot_general(from_row, sources, PLAIN, preferred_element_type=F32).astype(BF16)
    own = own_block()
    for n in range(FAR_CHUNKS):
        if copies and n % FAR_PER_COPY == 0:
            copies[n // FAR_PER_COPY].wait()
        d = pl.ds(n * FAR_CHUNK, FAR_CHUNK)
        source = jnp.concatenate([gathered[d, 3 * LEN * k : 3 * LEN * (k + 1)] for k in range(parts)], axis=0)
        matrix = jnp.concatenate([right[d, b].reshape(FAR_CHUNK * RANK, LEN) for b in range(3)], axis=1)
        c = summed(lax.dot_general(source, matrix, TRANS_B, preferred_element_type=F32), parts)
        c = jnp.where(own, c, 0.0)
        coefficients[n] = c.astype(BF16) if parts == 1 else jnp.concatenate(split3(c), axis=0)


def expand(parts, coefficients, left, out, payload, sems):
    copies = []
    for n in range(FAR_CHUNKS):
        d = pl.ds(n * FAR_CHUNK, FAR_CHUNK)
        matrix = jnp.concatenate([left[d, a].reshape(FAR_CHUNK * RANK, LEN) for a in range(3)], axis=1)
        result = summed(lax.dot_general(coefficients[n], matrix, PLAIN, preferred_element_type=F32), parts)
        for a in range(3):
            payload[d, a, :] = result[:, a * LEN : (a + 1) * LEN]
        if n % FAR_PER_COPY == FAR_PER_COPY - 1:
            copies.append(far_copy(payload, out, sems, n // FAR_PER_COPY))
            copies[-1].start()
    for copy in copies:
        copy.wait()


def far_sum(received, target):
    sub = lax.broadcasted_iota(jnp.int32, (8, LEN), 0).astype(F32)

    def some(n, totals):
        out = list(totals)
        for i in range(8):
            g = n * 8 + i
            hit = target(g) == sub
            for a in range(3):
                k = 3 * (i % 2) + a
                out[k] = out[k] + jnp.where(hit, received[g, a : a + 1, :], 0.0)
        return tuple(out)

    z = lax.fori_loop(0, DEVICES // 8, some, (jnp.zeros((8, LEN), F32),) * 6)
    return [z[a] + z[3 + a] for a in range(3)]


def flux(around, conductivity):
    pressure = around[3, 11:19, :]
    lane = lax.broadcasted_iota(jnp.int32, (8, LEN), 1)
    west = pltpu.roll(jnp.where(lane == LEN - 1, around[3, 1:9, :], pressure), 1, 1)
    east = pltpu.roll(jnp.where(lane == 0, around[3, 21:29, :], pressure), LEN - 1, 1)
    total = conductivity[0] * (around[3, 10:18, :] - pressure) + conductivity[1] * (around[3, 12:20, :] - pressure)
    return total + conductivity[2] * (west - pressure) + conductivity[3] * (east - pressure)


def image_of(vector, local, far_part):
    out = [vector[a] + local[a] + far_part[a] for a in range(3)]
    out[0] = out[0] - vector[3]
    return out + [vector[3] + vector[0] - local[3]]


def start_near(kernel_hbm, kernels, sems):
    for n in range(NEAR_CHUNKS):
        near_copy(kernel_hbm, kernels, sems, n).start()


def bring(
    source_hbm, target_hbm, vector_hbm, right_hbm, left_hbm, vector, source_row, target_row, right, left, sems
):
    pairs = (
        (source_hbm, source_row), (vector_hbm, vector), (target_hbm, target_row), (right_hbm, right), (left_hbm, left),
    )
    copies = [pltpu.make_async_copy(x, y, sems.at[i]) for i, (x, y) in enumerate(pairs)]
    for copy in copies:
        copy.start()
    for copy in copies:
        copy.wait()


def first_project(source_row, vector, right, coefficients, gathered):
    project(1, source_row[...], vector, coefficients, right, gathered, None)


def second_project(source_row, vector, right_hbm, coefficients, right, gathered, right_sems):
    rights = [far_copy(right_hbm, right, right_sems, n) for n in range(FAR_COPIES)]
    for copy in rights:
        copy.start()
    project(3, source_row[...], vector, coefficients, right, gathered, rights)


def first_expand(target_row, after, coefficients, left, out, payload, sems):
    payload[:, 3, :] = jnp.broadcast_to(target_row[...].astype(F32), (DEVICES, LEN)).T
    expand(1, coefficients, left, out, payload, sems)


def second_expand(row, after, coefficients, left, out, payload, sems):
    payload[:, 3, :] = jnp.broadcast_to(row[...], (DEVICES, LEN))
    expand(3, coefficients, left, out, payload, sems)


def edges(vector, swap_a, swap_b, after, out):
    strip, _ = place()
    even = lax.rem(strip, 2) == 0
    above = jnp.where(even, swap_b[:, ROWS - 1, :], swap_a[:, ROWS - 1, :])
    below = jnp.where(even, swap_a[:, 0, :], swap_b[:, 0, :])
    out[0:4] = vector[...]
    out[4, 0:4, :] = jnp.where(strip > 0, above, 0.0)
    out[4, 4:8, :] = jnp.where(strip < STRIPS - 1, below, 0.0)


def local_part(near_pair, conductivity, own, swap_a, swap_b, kernel_hbm, rounded, full, around, kernels, sems):
    start_near(kernel_hbm, kernels, sems)
    _, blk = place()
    even = lax.rem(blk, 2) == 0
    left = jnp.where(blk > 0, jnp.where(even, swap_b[...], swap_a[...]), 0.0)
    right = jnp.where(blk < BLKS - 1, jnp.where(even, swap_a[...], swap_b[...]), 0.0)
    for column, blocks in enumerate((left, own[...], right)):
        base = 10 * column
        around[:, base + 1 : base + 9, :] = blocks[0:4]
        around[:, base, :] = blocks[4, 0:4]
        around[:, base + 9, :] = blocks[4, 4:8]
    flux_sum = flux(around, conductivity)
    rounded[3] = flux_sum
    full[3] = flux_sum
    near_rounded, near_full = near(around, near_pair, kernels, lambda n: near_copy(kernel_hbm, kernels, sems, n).wait())
    for a in range(3):
        rounded[a] = near_rounded[:, a * LEN : (a + 1) * LEN]
        full[a] = near_full[:, a * LEN : (a + 1) * LEN]


def first_image(vector, local, received, image, far_part, row):
    arrived = far_sum(received, lambda g: received[g, 3:4, :])
    for a in range(3):
        far_part[a] = arrived[a]
    own = [vector[c] for c in range(4)]
    result = image_of(own, local, arrived)
    for c in range(4):
        image[c] = result[c]
    row[...] = dot_row([(own, own), (own, result), (result, result)])


def second_image(vector, image, local_one, local_two, target, received, far_one, first, image_two, scalars, rows):
    vv, vi, ii = totals(received[:, 3, :], 3)
    h = over_entries(vi)
    h0 = h[0]
    h0_pair = (h0, jnp.zeros_like(h0))
    square = pair_add(ii, pair_add(scaled(neg(pair_mul(h0_pair, vi)), 2.0), pair_mul(pair_mul(h0_pair, h0_pair), vv)))
    beta1 = jnp.sqrt(jnp.maximum(square[0], 0.0) / ENTRIES + EPSILON)
    h0_wide = jnp.broadcast_to(h0, (8, LEN))
    beta_wide = jnp.broadcast_to(beta1, (8, LEN))

    def of_first(of_image, of_vector):
        return (of_image - h0_wide * of_vector) / beta_wide

    start = [vector[c] for c in range(4)]
    own = [of_first(image[c], start[c]) for c in range(4)]
    for c in range(4):
        first[c] = own[c]
    arrived = far_sum(received, lambda g: target[g, 3:4, :])
    far_part = [of_first(arrived[a], far_one[a]) for a in range(3)]
    local = [of_first(local_two[c], local_one[c]) for c in range(4)]
    result = image_of(own, local, far_part)
    for c in range(4):
        image_two[c] = result[c]
    row = dot_row([(start, result), (own, result), (result, result), (start, start), (start, own), (own, own)])
    rows[...] = jnp.broadcast_to(row, (DEVICES, LEN))
    lane = lax.broadcasted_iota(jnp.int32, (1, LEN), 1)
    scalars[...] = jnp.where(lane == 0, h0, beta1)


def finish(vector, first, image, scalars, rows, krylov, hessenberg):
    si, fi, ii, ss, sf, ff = totals(rows[...], 6)
    g0, g1 = over_entries(si)[0], over_entries(fi)[0]
    zero = jnp.zeros_like(g0)
    p0, p1 = (g0, zero), (g1, zero)
    square = pair_add(ii, scaled(neg(pair_add(pair_mul(p0, si), pair_mul(p1, fi))), 2.0))
    cross = scaled(pair_mul(pair_mul(p0, p1), sf), 2.0)
    square = pair_add(square, pair_add(cross, pair_add(pair_mul(pair_mul(p0, p0), ss), pair_mul(pair_mul(p1, p1), ff))))
    beta2 = jnp.sqrt(jnp.maximum(square[0], 0.0) / ENTRIES + EPSILON)
    g0_wide, g1_wide, beta_wide = (jnp.broadcast_to(x, (8, LEN)) for x in (g0, g1, beta2))
    for c in range(4):
        krylov[0, c] = first[c]
        krylov[1, c] = (image[c] - g0_wide * vector[c] - g1_wide * first[c]) / beta_wide
    for i, value in enumerate((scalars[0, 0], scalars[0, 1], g0[0, 0], g1[0, 0], beta2[0, 0])):
        hessenberg[i] = value


def shape(*dims):
    return jax.ShapeDtypeStruct(dims, F32)


def limit(mib):
    return pltpu.CompilerParams(vmem_limit_bytes=mib * 1024 * 1024)


def in_hbm(x):
    return pltpu.with_memory_space_constraint(x, pltpu.HBM)


def exchange(x):
    return lax.all_to_all(x, ("strip", "blk"), 0, 0, tiled=True)


def swaps(x, axis, size):
    even = [(i, i ^ 1) for i in range(size)]
    odd = [(i, (i + 1) % size if i % 2 else (i - 1) % size) for i in range(size)]
    return lax.ppermute(x, axis, even), lax.ppermute(x, axis, odd)


def own_blocks(in_vmem, swap_a, swap_b, after):
    return pl.pallas_call(
        edges,
        out_shape=shape(5, ROWS, LEN),
        in_specs=[VMEM] * 3 + [ANY],
        out_specs=VMEM,
        compiler_params=limit(4),
        name="edges",
    )(in_vmem, swap_a, swap_b, after)


def local(vector, conductivity, near_kernel, near_pair, far_right, far_left, far_source_row, far_target_row):
    right = in_hbm(jnp.transpose(far_right[0], (0, 2, 1, 3)))
    left = in_hbm(jnp.transpose(far_left[0], (0, 2, 1, 3)))
    near_kernel = in_hbm(near_kernel)
    source_row, target_row = in_hbm(far_source_row), in_hbm(far_target_row)
    block, slots, line = shape(4, ROWS, LEN), shape(DEVICES, 4, LEN), shape(1, LEN)

    factors = jax.ShapeDtypeStruct((DEVICES, 3, RANK, LEN), BF16)
    far_buffer = pltpu.VMEM((DEVICES, 3, RANK, LEN), BF16)
    integers = jax.ShapeDtypeStruct((1, LEN), jnp.int32)
    cost = pl.CostEstimate(flops=2 * 10**8, bytes_accessed=10**7, transcendentals=0)

    def gathered_and_coefficients(parts):
        gathered = pltpu.VMEM((DEVICES, parts * 3 * LEN), BF16)
        return gathered, jax.ShapeDtypeStruct((FAR_CHUNKS, parts * FAR_CHUNK, FAR_CHUNK * RANK), BF16)

    expand_call = functools.partial(
        pl.pallas_call,
        out_shape=pltpu.HBM(slots.shape, F32),
        in_specs=[VMEM, ANY, VMEM, VMEM],
        out_specs=HBM,
        scratch_shapes=[pltpu.VMEM(slots.shape, F32), pltpu.SemaphoreType.DMA((FAR_COPIES,))],
        compiler_params=limit(4),
        cost_estimate=cost,
    )

    local_call = functools.partial(
        pl.pallas_call,
        local_part,
        out_shape=(block, block),
        in_specs=[SMEM, VMEM, VMEM, VMEM, VMEM, HBM],
        out_specs=(VMEM, VMEM),
        scratch_shapes=[
            pltpu.VMEM((4, HALO, LEN), F32),
            pltpu.VMEM((PAIRS, 3, 3, LEN, LEN), BF16),
            pltpu.SemaphoreType.DMA((NEAR_CHUNKS,)),
        ],
        compiler_params=limit(20),
        cost_estimate=pl.CostEstimate(flops=4 * 10**8, bytes_accessed=2 * 10**7, transcendentals=0),
        name="local_part",
    )

    swapped = swaps(vector, "strip", STRIPS)
    vector_vmem, source_row, target_row, right_vmem, left = pl.pallas_call(
        bring,
        out_shape=(block, integers, integers, factors, factors),
        in_specs=[HBM] * 5,
        out_specs=(VMEM,) * 5,
        scratch_shapes=[pltpu.SemaphoreType.DMA((5,))],
        compiler_params=limit(4),
        cost_estimate=cost,
        name="bring",
    )(source_row, target_row, in_hbm(vector), right, left)
    start = own_blocks(vector_vmem, *swapped, source_row)
    sides = swaps(start, "blk", BLKS)
    gathered, coefficients = gathered_and_coefficients(1)
    coefficients = pl.pallas_call(
        first_project,
        out_shape=coefficients,
        in_specs=[VMEM] * 3,
        out_specs=VMEM,
        scratch_shapes=[gathered],
        compiler_params=limit(4),
        cost_estimate=cost,
        name="first_project",
    )(source_row, start, right_vmem)
    payload = expand_call(first_expand, name="first_expand")(target_row, start, coefficients, left)
    payload, *sides = lax.optimization_barrier((payload, *sides))
    received_one = exchange(payload)
    rounded_one, local_one = local_call()(near_pair, conductivity, start, *sides, near_kernel)
    image, far_one, row = pl.pallas_call(
        first_image,
        out_shape=(block, shape(3, ROWS, LEN), line),
        in_specs=[VMEM] * 3,
        out_specs=(VMEM,) * 3,
        compiler_params=limit(4),
        name="first_image",
    )(start, rounded_one, received_one)
    swapped = swaps(image, "strip", STRIPS)
    own = own_blocks(image, *swapped, row)
    sides = swaps(own, "blk", BLKS)
    gathered, coefficients = gathered_and_coefficients(3)
    coefficients = pl.pallas_call(
        second_project,
        out_shape=coefficients,
        in_specs=[VMEM, VMEM, HBM],
        out_specs=VMEM,
        scratch_shapes=[far_buffer, gathered, pltpu.SemaphoreType.DMA((FAR_COPIES,))],
        compiler_params=limit(8),
        cost_estimate=cost,
        name="second_project",
    )(source_row, own, right)
    payload = expand_call(second_expand, name="second_expand")(row, own, coefficients, left)
    payload, *sides = lax.optimization_barrier((payload, *sides))
    received_two = exchange(payload)
    _, local_two = local_call()(near_pair, conductivity, own, *sides, near_kernel)
    first, image_two, scalars, rows = pl.pallas_call(
        second_image,
        out_shape=(block, block, line, shape(DEVICES, LEN)),
        in_specs=[VMEM] * 7,
        out_specs=(VMEM,) * 4,
        compiler_params=limit(4),
        name="second_image",
    )(start, image, local_one, local_two, received_one, received_two, far_one)
    rows = exchange(rows)
    krylov, hessenberg = pl.pallas_call(
        finish,
        out_shape=(shape(2, 4, ROWS, LEN), shape(5)),
        in_specs=[VMEM] * 5,
        out_specs=(VMEM, SMEM),
        compiler_params=limit(4),
        name="finish",
    )(start, first, image_two, scalars, rows)
    return krylov, hessenberg


def solution(mesh):
    in_specs = (
        P(None, "strip", "blk"),
        P(None, "strip", "blk"),
        P(("strip", "blk"), None, None, None, None),
        P(("strip", "blk")),
        P(("strip", "blk"), None, None, None, None),
        P(("strip", "blk"), None, None, None, None),
        P(("strip", "blk"), None),
        P(("strip", "blk"), None),
    )
    out_specs = (P(None, None, "strip", "blk"), P())
    return jax.shard_map(local, mesh=mesh, in_specs=in_specs, out_specs=out_specs, check_vma=False)
```

```python
import functools

import jax
import jax.numpy as jnp
from jax import lax
from jax.experimental import pallas as pl
from jax.experimental.pallas import tpu as pltpu
from jax.sharding import PartitionSpec as P

EPSILON = 1e-06
STRIPS, BLKS, DEVICES = 8, 16, 128
ROWS, LEN, RANK, PAIRS = 8, 128, 32, 48
ENTRIES = float(4 * STRIPS * ROWS * BLKS * LEN)
HALO = 32
NEAR_CHUNK = 8
NEAR_CHUNKS = PAIRS // NEAR_CHUNK
FAR_CHUNK = 16
FAR_CHUNKS = DEVICES // FAR_CHUNK
FAR_PER_COPY = 2
FAR_COPIES = FAR_CHUNKS // FAR_PER_COPY
BF16, F32 = jnp.bfloat16, jnp.float32
TRANS_B = (((1,), (1,)), ((), ()))
PLAIN = (((1,), (0,)), ((), ()))
VMEM = pl.BlockSpec(memory_space=pltpu.VMEM)
SMEM = pl.BlockSpec(memory_space=pltpu.SMEM)
ANY = pl.BlockSpec(memory_space=pl.ANY)
HBM = pl.BlockSpec(memory_space=pltpu.HBM)


def two_sum(a, b):
    s = a + b
    t = s - a
    return s, (a - (s - t)) + (b - t)


def halves(a):
    c = a * 4097.0
    hi = c - (c - a)
    return hi, a - hi


def two_prod(a, b):
    p = a * b
    ah, al = halves(a)
    bh, bl = halves(b)
    return p, ((ah * bh - p) + ah * bl + al * bh) + al * bl


def pair_add(x, y):
    s, e = two_sum(x[0], y[0])
    return two_sum(s, e + (x[1] + y[1]))


def pair_mul(x, y):
    p, e = two_prod(x[0], y[0])
    return two_sum(p, e + (x[0] * y[1] + x[1] * y[0]))


def neg(x):
    return -x[0], -x[1]


def scaled(x, power_of_two):
    return x[0] * power_of_two, x[1] * power_of_two


def dot_row(pairs):
    sub = lax.broadcasted_iota(jnp.int32, (8, LEN), 0)
    high = jnp.zeros((8, LEN), F32)
    low = jnp.zeros((8, LEN), F32)
    for k, (a, b) in enumerate(pairs):
        s, e = two_prod(a[0], b[0])
        for c in range(1, 4):
            s, e = pair_add((s, e), two_prod(a[c], b[c]))
        for step in (4, 2, 1):
            s, e = pair_add((s, e), (pltpu.roll(s, step, 0), pltpu.roll(e, step, 0)))
        high = jnp.where(sub == k, s, high)
        low = jnp.where(sub == k, e, low)
    pad = jnp.zeros((LEN - 16, LEN), F32)
    turned = jnp.concatenate([high, low, pad], axis=0).T
    s, e = column_sums(turned)
    return s + pltpu.roll(e, 16, 1)


def column_sums(x):
    parts = [(x[8 * i : 8 * i + 8], jnp.zeros((8, LEN), F32)) for i in range(16)]
    while len(parts) > 1:
        parts = [pair_add(parts[i], parts[i + 1]) for i in range(0, len(parts), 2)]
    s, e = parts[0]
    for step in (4, 2, 1):
        s, e = pair_add((s, e), (pltpu.roll(s, step, 0), pltpu.roll(e, step, 0)))
    return s[0:1], e[0:1]


def totals(rows, count):
    s, e = column_sums(rows)
    low = e + pltpu.roll(s, LEN - 8, 1) + pltpu.roll(s, LEN - 16, 1)
    s, low = two_sum(s, low)
    return [(s[0:1, k : k + 1], low[0:1, k : k + 1]) for k in range(count)]


def over_entries(x):
    return scaled(x, 1.0 / ENTRIES)


def place():
    strip, blk = lax.axis_index("strip"), lax.axis_index("blk")
    return strip, blk


def near(around, near_pair, kernels, wait):
    sub = lax.broadcasted_iota(jnp.int32, (8, LEN), 0)

    def chunk(n, total):
        wait(n)
        rows, matrices = [], []
        for i in range(NEAR_CHUNK):
            p = n * NEAR_CHUNK + i
            code = near_pair[p]
            t = code // 9
            k = code - 9 * t
            up = k // 3
            source = (k - 3 * up) * 10 + t + up
            for b in range(3):
                rows.append(jnp.where(sub == t, around[b, pl.ds(source, 1), :], 0.0))
                matrices.append(kernels[p, :, b].reshape(3 * LEN, LEN))
        left = jnp.concatenate(split3(jnp.concatenate(rows, axis=1)), axis=0)
        matrix = jnp.concatenate(matrices, axis=1)
        return total + lax.dot_general(left, matrix, TRANS_B, preferred_element_type=F32)

    total = lax.fori_loop(0, NEAR_CHUNKS, chunk, jnp.zeros((24, 3 * LEN), F32))
    return total[0:8], total[0:8] + (total[8:16] + total[16:24])


def near_copy(kernel_hbm, kernels, sems, n):
    part = pl.ds(n * NEAR_CHUNK, NEAR_CHUNK)
    return pltpu.make_async_copy(kernel_hbm.at[part], kernels.at[part], sems.at[n])


def far_copy(hbm, buffer, sems, n):
    part = pl.ds(n * FAR_CHUNK * FAR_PER_COPY, FAR_CHUNK * FAR_PER_COPY)
    return pltpu.make_async_copy(hbm.at[part], buffer.at[part], sems.at[n])


def split3(x):
    a = x.astype(BF16)
    rest = x - a.astype(F32)
    b = rest.astype(BF16)
    c = (rest - b.astype(F32)).astype(BF16)
    return a, b, c


def own_block():
    sub = lax.broadcasted_iota(jnp.int32, (FAR_CHUNK, FAR_CHUNK * RANK), 0)
    lane = lax.broadcasted_iota(jnp.int32, (FAR_CHUNK, FAR_CHUNK * RANK), 1)
    return lane // RANK == sub


def summed(x, parts):
    if parts == 1:
        return x
    return x[0:FAR_CHUNK] + (x[FAR_CHUNK : 2 * FAR_CHUNK] + x[2 * FAR_CHUNK :])


def project(parts, source_row, vector, coefficients, right, gathered):
    pieces = [[x.astype(BF16)] if parts == 1 else split3(x) for x in (vector[b] for b in range(3))]
    below = jnp.zeros((LEN - ROWS, LEN), F32)
    sources = [jnp.concatenate([pieces[b][k].astype(F32), below], axis=0).astype(BF16) for k in range(parts) for b in range(3)]
    sources = jnp.concatenate(sources, axis=1)
    row = lax.broadcasted_iota(jnp.int32, (LEN, LEN), 0)
    from_row = jnp.where(row == source_row, 1.0, 0.0).T.astype(BF16)
    gathered[...] = lax.dot_general(from_row, sources, PLAIN, preferred_element_type=F32).astype(BF16)
    own = own_block()
    for n in range(FAR_CHUNKS):
        d = pl.ds(n * FAR_CHUNK, FAR_CHUNK)
        source = jnp.concatenate([gathered[d, 3 * LEN * k : 3 * LEN * (k + 1)] for k in range(parts)], axis=0)
        matrix = jnp.concatenate([right[d, b].reshape(FAR_CHUNK * RANK, LEN) for b in range(3)], axis=1)
        c = summed(lax.dot_general(source, matrix, TRANS_B, preferred_element_type=F32), parts)
        c = jnp.where(own, c, 0.0)
        coefficients[n] = c.astype(BF16) if parts == 1 else jnp.concatenate(split3(c), axis=0)


def expand(parts, coefficients, left, out, payload, sems):
    copies = []
    for n in range(FAR_CHUNKS):
        d = pl.ds(n * FAR_CHUNK, FAR_CHUNK)
        matrix = jnp.concatenate([left[d, a].reshape(FAR_CHUNK * RANK, LEN) for a in range(3)], axis=1)
        result = summed(lax.dot_general(coefficients[n], matrix, PLAIN, preferred_element_type=F32), parts)
        for a in range(3):
            payload[d, a, :] = result[:, a * LEN : (a + 1) * LEN]
        if n % FAR_PER_COPY == FAR_PER_COPY - 1:
            copies.append(far_copy(payload, out, sems, n // FAR_PER_COPY))
            copies[-1].start()
    for copy in copies:
        copy.wait()


def far_sum(received, target):
    sub = lax.broadcasted_iota(jnp.int32, (8, LEN), 0).astype(F32)

    def some(n, totals):
        out = list(totals)
        for i in range(8):
            g = n * 8 + i
            hit = target(g) == sub
            for a in range(3):
                k = 3 * (i % 2) + a
                out[k] = out[k] + jnp.where(hit, received[g, a : a + 1, :], 0.0)
        return tuple(out)

    z = lax.fori_loop(0, DEVICES // 8, some, (jnp.zeros((8, LEN), F32),) * 6)
    return [z[a] + z[3 + a] for a in range(3)]


def flux(around, conductivity):
    pressure = around[3, 11:19, :]
    lane = lax.broadcasted_iota(jnp.int32, (8, LEN), 1)
    west = pltpu.roll(jnp.where(lane == LEN - 1, around[3, 1:9, :], pressure), 1, 1)
    east = pltpu.roll(jnp.where(lane == 0, around[3, 21:29, :], pressure), LEN - 1, 1)
    total = conductivity[0] * (around[3, 10:18, :] - pressure) + conductivity[1] * (around[3, 12:20, :] - pressure)
    return total + conductivity[2] * (west - pressure) + conductivity[3] * (east - pressure)


def image_of(vector, local, far_part):
    out = [vector[a] + local[a] + far_part[a] for a in range(3)]
    out[0] = out[0] - vector[3]
    return out + [vector[3] + vector[0] - local[3]]


def start_near(kernel_hbm, kernels, sems):
    for n in range(NEAR_CHUNKS):
        near_copy(kernel_hbm, kernels, sems, n).start()


def bring(source_hbm, target_hbm, vector_hbm, right_hbm, vector, source_row, target_row, right, sems):
    pairs = ((source_hbm, source_row), (vector_hbm, vector), (target_hbm, target_row), (right_hbm, right))
    copies = [pltpu.make_async_copy(x, y, sems.at[i]) for i, (x, y) in enumerate(pairs)]
    for copy in copies:
        copy.start()
    for copy in copies:
        copy.wait()


def bring_right(after, right_hbm, right, sem):
    copy = pltpu.make_async_copy(right_hbm, right, sem)
    copy.start()
    copy.wait()


def first_project(source_row, vector, right, left_hbm, coefficients, left, gathered, sem):
    copy = pltpu.make_async_copy(left_hbm, left, sem)
    copy.start()
    project(1, source_row[...], vector, coefficients, right, gathered)
    copy.wait()


def second_project(source_row, vector, right, coefficients, gathered):
    project(3, source_row[...], vector, coefficients, right, gathered)


def first_expand(target_row, after, coefficients, left, out, payload, sems):
    payload[:, 3, :] = jnp.broadcast_to(target_row[...].astype(F32), (DEVICES, LEN)).T
    expand(1, coefficients, left, out, payload, sems)


def second_expand(row, after, coefficients, left, out, payload, sems):
    payload[:, 3, :] = jnp.broadcast_to(row[...], (DEVICES, LEN))
    expand(3, coefficients, left, out, payload, sems)


def edges(vector, swap_a, swap_b, after, out):
    strip, _ = place()
    even = lax.rem(strip, 2) == 0
    above = jnp.where(even, swap_b[:, ROWS - 1, :], swap_a[:, ROWS - 1, :])
    below = jnp.where(even, swap_a[:, 0, :], swap_b[:, 0, :])
    out[0:4] = vector[...]
    out[4, 0:4, :] = jnp.where(strip > 0, above, 0.0)
    out[4, 4:8, :] = jnp.where(strip < STRIPS - 1, below, 0.0)


def local_part(near_pair, conductivity, own, swap_a, swap_b, kernel_hbm, rounded, full, around, kernels, sems):
    start_near(kernel_hbm, kernels, sems)
    _, blk = place()
    even = lax.rem(blk, 2) == 0
    left = jnp.where(blk > 0, jnp.where(even, swap_b[...], swap_a[...]), 0.0)
    right = jnp.where(blk < BLKS - 1, jnp.where(even, swap_a[...], swap_b[...]), 0.0)
    for column, blocks in enumerate((left, own[...], right)):
        base = 10 * column
        around[:, base + 1 : base + 9, :] = blocks[0:4]
        around[:, base, :] = blocks[4, 0:4]
        around[:, base + 9, :] = blocks[4, 4:8]
    flux_sum = flux(around, conductivity)
    rounded[3] = flux_sum
    full[3] = flux_sum
    near_rounded, near_full = near(around, near_pair, kernels, lambda n: near_copy(kernel_hbm, kernels, sems, n).wait())
    for a in range(3):
        rounded[a] = near_rounded[:, a * LEN : (a + 1) * LEN]
        full[a] = near_full[:, a * LEN : (a + 1) * LEN]


def first_image(vector, local, received, image, far_part, row):
    arrived = far_sum(received, lambda g: received[g, 3:4, :])
    for a in range(3):
        far_part[a] = arrived[a]
    own = [vector[c] for c in range(4)]
    result = image_of(own, local, arrived)
    for c in range(4):
        image[c] = result[c]
    row[...] = dot_row([(own, own), (own, result), (result, result)])


def second_image(vector, image, local_one, local_two, target, received, far_one, first, image_two, scalars, rows):
    vv, vi, ii = totals(received[:, 3, :], 3)
    h = over_entries(vi)
    h0 = h[0]
    h0_pair = (h0, jnp.zeros_like(h0))
    square = pair_add(ii, pair_add(scaled(neg(pair_mul(h0_pair, vi)), 2.0), pair_mul(pair_mul(h0_pair, h0_pair), vv)))
    beta1 = jnp.sqrt(jnp.maximum(square[0], 0.0) / ENTRIES + EPSILON)
    h0_wide = jnp.broadcast_to(h0, (8, LEN))
    beta_wide = jnp.broadcast_to(beta1, (8, LEN))

    def of_first(of_image, of_vector):
        return (of_image - h0_wide * of_vector) / beta_wide

    start = [vector[c] for c in range(4)]
    own = [of_first(image[c], start[c]) for c in range(4)]
    for c in range(4):
        first[c] = own[c]
    arrived = far_sum(received, lambda g: target[g, 3:4, :])
    far_part = [of_first(arrived[a], far_one[a]) for a in range(3)]
    local = [of_first(local_two[c], local_one[c]) for c in range(4)]
    result = image_of(own, local, far_part)
    for c in range(4):
        image_two[c] = result[c]
    row = dot_row([(start, result), (own, result), (result, result), (start, start), (start, own), (own, own)])
    rows[...] = jnp.broadcast_to(row, (DEVICES, LEN))
    lane = lax.broadcasted_iota(jnp.int32, (1, LEN), 1)
    scalars[...] = jnp.where(lane == 0, h0, beta1)


def finish(vector, first, image, scalars, rows, krylov, hessenberg):
    si, fi, ii, ss, sf, ff = totals(rows[...], 6)
    g0, g1 = over_entries(si)[0], over_entries(fi)[0]
    zero = jnp.zeros_like(g0)
    p0, p1 = (g0, zero), (g1, zero)
    square = pair_add(ii, scaled(neg(pair_add(pair_mul(p0, si), pair_mul(p1, fi))), 2.0))
    cross = scaled(pair_mul(pair_mul(p0, p1), sf), 2.0)
    square = pair_add(square, pair_add(cross, pair_add(pair_mul(pair_mul(p0, p0), ss), pair_mul(pair_mul(p1, p1), ff))))
    beta2 = jnp.sqrt(jnp.maximum(square[0], 0.0) / ENTRIES + EPSILON)
    g0_wide, g1_wide, beta_wide = (jnp.broadcast_to(x, (8, LEN)) for x in (g0, g1, beta2))
    for c in range(4):
        krylov[0, c] = first[c]
        krylov[1, c] = (image[c] - g0_wide * vector[c] - g1_wide * first[c]) / beta_wide
    for i, value in enumerate((scalars[0, 0], scalars[0, 1], g0[0, 0], g1[0, 0], beta2[0, 0])):
        hessenberg[i] = value


def shape(*dims):
    return jax.ShapeDtypeStruct(dims, F32)


def limit(mib):
    return pltpu.CompilerParams(vmem_limit_bytes=mib * 1024 * 1024)


def in_hbm(x):
    return pltpu.with_memory_space_constraint(x, pltpu.HBM)


def exchange(x):
    return lax.all_to_all(x, ("strip", "blk"), 0, 0, tiled=True)


def swaps(x, axis, size):
    even = [(i, i ^ 1) for i in range(size)]
    odd = [(i, (i + 1) % size if i % 2 else (i - 1) % size) for i in range(size)]
    return lax.ppermute(x, axis, even), lax.ppermute(x, axis, odd)


def own_blocks(in_vmem, swap_a, swap_b, after):
    return pl.pallas_call(
        edges,
        out_shape=shape(5, ROWS, LEN),
        in_specs=[VMEM] * 3 + [ANY],
        out_specs=VMEM,
        compiler_params=limit(4),
        name="edges",
    )(in_vmem, swap_a, swap_b, after)


def local(vector, conductivity, near_kernel, near_pair, far_right, far_left, far_source_row, far_target_row):
    right = in_hbm(jnp.transpose(far_right[0], (0, 2, 1, 3)))
    left = in_hbm(jnp.transpose(far_left[0], (0, 2, 1, 3)))
    near_kernel = in_hbm(near_kernel)
    source_row, target_row = in_hbm(far_source_row), in_hbm(far_target_row)
    block, slots, line = shape(4, ROWS, LEN), shape(DEVICES, 4, LEN), shape(1, LEN)

    factors = jax.ShapeDtypeStruct((DEVICES, 3, RANK, LEN), BF16)
    integers = jax.ShapeDtypeStruct((1, LEN), jnp.int32)
    cost = pl.CostEstimate(flops=2 * 10**8, bytes_accessed=10**7, transcendentals=0)

    def gathered_and_coefficients(parts):
        gathered = pltpu.VMEM((DEVICES, parts * 3 * LEN), BF16)
        return gathered, jax.ShapeDtypeStruct((FAR_CHUNKS, parts * FAR_CHUNK, FAR_CHUNK * RANK), BF16)

    expand_call = functools.partial(
        pl.pallas_call,
        out_shape=pltpu.HBM(slots.shape, F32),
        in_specs=[VMEM, ANY, VMEM, VMEM],
        out_specs=HBM,
        scratch_shapes=[pltpu.VMEM(slots.shape, F32), pltpu.SemaphoreType.DMA((FAR_COPIES,))],
        compiler_params=limit(4),
        cost_estimate=cost,
    )

    local_call = functools.partial(
        pl.pallas_call,
        local_part,
        out_shape=(block, block),
        in_specs=[SMEM, VMEM, VMEM, VMEM, VMEM, HBM],
        out_specs=(VMEM, VMEM),
        scratch_shapes=[
            pltpu.VMEM((4, HALO, LEN), F32),
            pltpu.VMEM((PAIRS, 3, 3, LEN, LEN), BF16),
            pltpu.SemaphoreType.DMA((NEAR_CHUNKS,)),
        ],
        compiler_params=limit(20),
        cost_estimate=pl.CostEstimate(flops=4 * 10**8, bytes_accessed=2 * 10**7, transcendentals=0),
        name="local_part",
    )

    swapped = swaps(vector, "strip", STRIPS)
    vector_vmem, source_row, target_row, right_vmem = pl.pallas_call(
        bring,
        out_shape=(block, integers, integers, factors),
        in_specs=[HBM] * 4,
        out_specs=(VMEM,) * 4,
        scratch_shapes=[pltpu.SemaphoreType.DMA((4,))],
        compiler_params=limit(4),
        cost_estimate=cost,
        name="bring",
    )(source_row, target_row, in_hbm(vector), right)
    start = own_blocks(vector_vmem, *swapped, source_row)
    sides = swaps(start, "blk", BLKS)
    gathered, coefficients = gathered_and_coefficients(1)
    coefficients, left = pl.pallas_call(
        first_project,
        out_shape=(coefficients, factors),
        in_specs=[VMEM, VMEM, VMEM, HBM],
        out_specs=(VMEM, VMEM),
        scratch_shapes=[gathered, pltpu.SemaphoreType.DMA],
        compiler_params=limit(4),
        cost_estimate=cost,
        name="first_project",
    )(source_row, start, right_vmem, left)
    payload = expand_call(first_expand, name="first_expand")(target_row, start, coefficients, left)
    payload, *sides = lax.optimization_barrier((payload, *sides))
    received_one = exchange(payload)
    rounded_one, local_one = local_call()(near_pair, conductivity, start, *sides, near_kernel)
    image, far_one, row = pl.pallas_call(
        first_image,
        out_shape=(block, shape(3, ROWS, LEN), line),
        in_specs=[VMEM] * 3,
        out_specs=(VMEM,) * 3,
        compiler_params=limit(4),
        name="first_image",
    )(start, rounded_one, received_one)
    swapped = swaps(image, "strip", STRIPS)
    right_vmem = pl.pallas_call(
        bring_right,
        out_shape=factors,
        in_specs=[ANY, HBM],
        out_specs=VMEM,
        scratch_shapes=[pltpu.SemaphoreType.DMA],
        compiler_params=limit(4),
        cost_estimate=cost,
        name="bring_right",
    )(image, right)
    own = own_blocks(image, *swapped, right_vmem)
    sides = swaps(own, "blk", BLKS)
    gathered, coefficients = gathered_and_coefficients(3)
    coefficients = pl.pallas_call(
        second_project,
        out_shape=coefficients,
        in_specs=[VMEM] * 3,
        out_specs=VMEM,
        scratch_shapes=[gathered],
        compiler_params=limit(4),
        cost_estimate=cost,
        name="second_project",
    )(source_row, own, right_vmem)
    payload = expand_call(second_expand, name="second_expand")(row, own, coefficients, left)
    payload, *sides = lax.optimization_barrier((payload, *sides))
    received_two = exchange(payload)
    _, local_two = local_call()(near_pair, conductivity, own, *sides, near_kernel)
    first, image_two, scalars, rows = pl.pallas_call(
        second_image,
        out_shape=(block, block, line, shape(DEVICES, LEN)),
        in_specs=[VMEM] * 7,
        out_specs=(VMEM,) * 4,
        compiler_params=limit(4),
        name="second_image",
    )(start, image, local_one, local_two, received_one, received_two, far_one)
    rows = exchange(rows)
    krylov, hessenberg = pl.pallas_call(
        finish,
        out_shape=(shape(2, 4, ROWS, LEN), shape(5)),
        in_specs=[VMEM] * 5,
        out_specs=(VMEM, SMEM),
        compiler_params=limit(4),
        name="finish",
    )(start, first, image_two, scalars, rows)
    return krylov, hessenberg


def solution(mesh):
    in_specs = (
        P(None, "strip", "blk"),
        P(None, "strip", "blk"),
        P(("strip", "blk"), None, None, None, None),
        P(("strip", "blk")),
        P(("strip", "blk"), None, None, None, None),
        P(("strip", "blk"), None, None, None, None),
        P(("strip", "blk"), None),
        P(("strip", "blk"), None),
    )
    out_specs = (P(None, None, "strip", "blk"), P())
    return jax.shard_map(local, mesh=mesh, in_specs=in_specs, out_specs=out_specs, check_vma=False)
```

```python
import functools

import jax
import jax.numpy as jnp
from jax import lax
from jax.experimental import pallas as pl
from jax.experimental.pallas import tpu as pltpu
from jax.sharding import PartitionSpec as P

EPSILON = 1e-06
STRIPS, BLKS, DEVICES = 8, 16, 128
ROWS, LEN, RANK, PAIRS = 8, 128, 32, 48
ENTRIES = float(4 * STRIPS * ROWS * BLKS * LEN)
HALO = 32
NEAR_CHUNK = 8
NEAR_CHUNKS = PAIRS // NEAR_CHUNK
FAR_CHUNK = 16
FAR_CHUNKS = DEVICES // FAR_CHUNK
FAR_PER_COPY = 2
FAR_COPIES = FAR_CHUNKS // FAR_PER_COPY
BF16, F32 = jnp.bfloat16, jnp.float32
TRANS_B = (((1,), (1,)), ((), ()))
PLAIN = (((1,), (0,)), ((), ()))
VMEM = pl.BlockSpec(memory_space=pltpu.VMEM)
SMEM = pl.BlockSpec(memory_space=pltpu.SMEM)
ANY = pl.BlockSpec(memory_space=pl.ANY)
HBM = pl.BlockSpec(memory_space=pltpu.HBM)


def two_sum(a, b):
    s = a + b
    t = s - a
    return s, (a - (s - t)) + (b - t)


def halves(a):
    c = a * 4097.0
    hi = c - (c - a)
    return hi, a - hi


def two_prod(a, b):
    p = a * b
    ah, al = halves(a)
    bh, bl = halves(b)
    return p, ((ah * bh - p) + ah * bl + al * bh) + al * bl


def pair_add(x, y):
    s, e = two_sum(x[0], y[0])
    return two_sum(s, e + (x[1] + y[1]))


def loose_add(x, y):
    s, e = two_sum(x[0], y[0])
    return s, e + (x[1] + y[1])


def pair_mul(x, y):
    p, e = two_prod(x[0], y[0])
    return two_sum(p, e + (x[0] * y[1] + x[1] * y[0]))


def neg(x):
    return -x[0], -x[1]


def scaled(x, power_of_two):
    return x[0] * power_of_two, x[1] * power_of_two


def dot_row(pairs):
    sub = lax.broadcasted_iota(jnp.int32, (8, LEN), 0)
    high = jnp.zeros((8, LEN), F32)
    low = jnp.zeros((8, LEN), F32)
    for k, (a, b) in enumerate(pairs):
        s, e = two_prod(a[0], b[0])
        for c in range(1, 4):
            s, e = loose_add((s, e), two_prod(a[c], b[c]))
        for step in (4, 2, 1):
            s, e = loose_add((s, e), (pltpu.roll(s, step, 0), pltpu.roll(e, step, 0)))
        s, e = two_sum(s, e)
        high = jnp.where(sub == k, s, high)
        low = jnp.where(sub == k, e, low)
    pad = jnp.zeros((LEN - 16, LEN), F32)
    turned = jnp.concatenate([high, low, pad], axis=0).T
    s, e = column_sums(turned)
    return s + pltpu.roll(e, 16, 1)


def column_sums(x):
    parts = [(x[8 * i : 8 * i + 8], jnp.zeros((8, LEN), F32)) for i in range(16)]
    while len(parts) > 1:
        parts = [loose_add(parts[i], parts[i + 1]) for i in range(0, len(parts), 2)]
    s, e = parts[0]
    for step in (4, 2, 1):
        s, e = loose_add((s, e), (pltpu.roll(s, step, 0), pltpu.roll(e, step, 0)))
    s, e = two_sum(s[0:1], e[0:1])
    return s, e


def totals(rows, count):
    s, e = column_sums(rows)
    low = e + pltpu.roll(s, LEN - 8, 1) + pltpu.roll(s, LEN - 16, 1)
    s, low = two_sum(s, low)
    return [(s[0:1, k : k + 1], low[0:1, k : k + 1]) for k in range(count)]


def over_entries(x):
    return scaled(x, 1.0 / ENTRIES)


def place():
    strip, blk = lax.axis_index("strip"), lax.axis_index("blk")
    return strip, blk


def near(around, near_pair, kernels, wait):
    sub = lax.broadcasted_iota(jnp.int32, (8, LEN), 0)

    def chunk(n, total):
        wait(n)
        rows, matrices = [], []
        for i in range(NEAR_CHUNK):
            p = n * NEAR_CHUNK + i
            code = near_pair[p]
            t = code // 9
            k = code - 9 * t
            up = k // 3
            source = (k - 3 * up) * 10 + t + up
            for b in range(3):
                rows.append(jnp.where(sub == t, around[b, pl.ds(source, 1), :], 0.0))
                matrices.append(kernels[p, :, b].reshape(3 * LEN, LEN))
        left = jnp.concatenate(split3(jnp.concatenate(rows, axis=1)), axis=0)
        matrix = jnp.concatenate(matrices, axis=1)
        return total + lax.dot_general(left, matrix, TRANS_B, preferred_element_type=F32)

    total = lax.fori_loop(0, NEAR_CHUNKS, chunk, jnp.zeros((24, 3 * LEN), F32))
    return total[0:8], total[0:8] + (total[8:16] + total[16:24])


def near_copy(kernel_hbm, kernels, sems, n):
    part = pl.ds(n * NEAR_CHUNK, NEAR_CHUNK)
    return pltpu.make_async_copy(kernel_hbm.at[part], kernels.at[part], sems.at[n])


def far_copy(hbm, buffer, sems, n):
    part = pl.ds(n * FAR_CHUNK * FAR_PER_COPY, FAR_CHUNK * FAR_PER_COPY)
    return pltpu.make_async_copy(hbm.at[part], buffer.at[part], sems.at[n])


def split3(x):
    a = x.astype(BF16)
    rest = x - a.astype(F32)
    b = rest.astype(BF16)
    c = (rest - b.astype(F32)).astype(BF16)
    return a, b, c


def own_block():
    sub = lax.broadcasted_iota(jnp.int32, (FAR_CHUNK, FAR_CHUNK * RANK), 0)
    lane = lax.broadcasted_iota(jnp.int32, (FAR_CHUNK, FAR_CHUNK * RANK), 1)
    return lane // RANK == sub


def summed(x, parts):
    if parts == 1:
        return x
    return x[0:FAR_CHUNK] + (x[FAR_CHUNK : 2 * FAR_CHUNK] + x[2 * FAR_CHUNK :])


def project(parts, source_row, vector, coefficients, right, gathered):
    pieces = [[x.astype(BF16)] if parts == 1 else split3(x) for x in (vector[b] for b in range(3))]
    below = jnp.zeros((LEN - ROWS, LEN), F32)
    sources = [jnp.concatenate([pieces[b][k].astype(F32), below], axis=0).astype(BF16) for k in range(parts) for b in range(3)]
    sources = jnp.concatenate(sources, axis=1)
    row = lax.broadcasted_iota(jnp.int32, (LEN, LEN), 0)
    from_row = jnp.where(row == source_row, 1.0, 0.0).T.astype(BF16)
    gathered[...] = lax.dot_general(from_row, sources, PLAIN, preferred_element_type=F32).astype(BF16)
    own = own_block()
    for n in range(FAR_CHUNKS):
        d = pl.ds(n * FAR_CHUNK, FAR_CHUNK)
        source = jnp.concatenate([gathered[d, 3 * LEN * k : 3 * LEN * (k + 1)] for k in range(parts)], axis=0)
        matrix = jnp.concatenate([right[d, b].reshape(FAR_CHUNK * RANK, LEN) for b in range(3)], axis=1)
        c = summed(lax.dot_general(source, matrix, TRANS_B, preferred_element_type=F32), parts)
        c = jnp.where(own, c, 0.0)
        coefficients[n] = c.astype(BF16) if parts == 1 else jnp.concatenate(split3(c), axis=0)


def expand(parts, coefficients, left, out, payload, sems):
    copies = []
    for n in range(FAR_CHUNKS):
        d = pl.ds(n * FAR_CHUNK, FAR_CHUNK)
        matrix = jnp.concatenate([left[d, a].reshape(FAR_CHUNK * RANK, LEN) for a in range(3)], axis=1)
        result = summed(lax.dot_general(coefficients[n], matrix, PLAIN, preferred_element_type=F32), parts)
        for a in range(3):
            payload[d, a, :] = result[:, a * LEN : (a + 1) * LEN]
        if n % FAR_PER_COPY == FAR_PER_COPY - 1:
            copies.append(far_copy(payload, out, sems, n // FAR_PER_COPY))
            copies[-1].start()
    for copy in copies:
        copy.wait()


def far_sum(received, target):
    sub = lax.broadcasted_iota(jnp.int32, (8, LEN), 0).astype(F32)

    def some(n, totals):
        out = list(totals)
        for i in range(8):
            g = n * 8 + i
            hit = target(g) == sub
            for a in range(3):
                k = 3 * (i % 2) + a
                out[k] = out[k] + jnp.where(hit, received[g, a : a + 1, :], 0.0)
        return tuple(out)

    z = lax.fori_loop(0, DEVICES // 8, some, (jnp.zeros((8, LEN), F32),) * 6)
    return [z[a] + z[3 + a] for a in range(3)]


def flux(around, conductivity):
    pressure = around[3, 11:19, :]
    lane = lax.broadcasted_iota(jnp.int32, (8, LEN), 1)
    west = pltpu.roll(jnp.where(lane == LEN - 1, around[3, 1:9, :], pressure), 1, 1)
    east = pltpu.roll(jnp.where(lane == 0, around[3, 21:29, :], pressure), LEN - 1, 1)
    total = conductivity[0] * (around[3, 10:18, :] - pressure) + conductivity[1] * (around[3, 12:20, :] - pressure)
    return total + conductivity[2] * (west - pressure) + conductivity[3] * (east - pressure)


def image_of(vector, local, far_part):
    out = [vector[a] + local[a] + far_part[a] for a in range(3)]
    out[0] = out[0] - vector[3]
    return out + [vector[3] + vector[0] - local[3]]


def start_near(kernel_hbm, kernels, sems):
    for n in range(NEAR_CHUNKS):
        near_copy(kernel_hbm, kernels, sems, n).start()


def bring(source_hbm, target_hbm, vector_hbm, right_hbm, vector, source_row, target_row, right, sems):
    pairs = ((source_hbm, source_row), (vector_hbm, vector), (target_hbm, target_row), (right_hbm, right))
    copies = [pltpu.make_async_copy(x, y, sems.at[i]) for i, (x, y) in enumerate(pairs)]
    for copy in copies:
        copy.start()
    for copy in copies:
        copy.wait()


def bring_right(after, right_hbm, right, sem):
    copy = pltpu.make_async_copy(right_hbm, right, sem)
    copy.start()
    copy.wait()


def first_project(source_row, vector, right, left_hbm, coefficients, left, gathered, sem):
    copy = pltpu.make_async_copy(left_hbm, left, sem)
    copy.start()
    project(1, source_row[...], vector, coefficients, right, gathered)
    copy.wait()


def second_project(source_row, vector, right, coefficients, gathered):
    project(3, source_row[...], vector, coefficients, right, gathered)


def first_expand(target_row, after, coefficients, left, out, payload, sems):
    payload[:, 3, :] = jnp.broadcast_to(target_row[...].astype(F32), (DEVICES, LEN)).T
    expand(1, coefficients, left, out, payload, sems)


def second_expand(vector, image, coefficients, left, out, payload, sems):
    start = [vector[c] for c in range(4)]
    own = [image[c] for c in range(4)]
    row = dot_row([(start, start), (start, own), (own, own)])
    payload[:, 3, :] = jnp.broadcast_to(row, (DEVICES, LEN))
    expand(3, coefficients, left, out, payload, sems)


def edges(vector, swap_a, swap_b, after, out):
    strip, _ = place()
    even = lax.rem(strip, 2) == 0
    if len(swap_a.shape) == 3:
        above = jnp.where(even, swap_b[:, ROWS - 1, :], swap_a[:, ROWS - 1, :])
        below = jnp.where(even, swap_a[:, 0, :], swap_b[:, 0, :])
    else:
        above = jnp.where(even, swap_b[...], swap_a[...])
        below = jnp.where(even, swap_a[...], swap_b[...])
    out[0:4] = vector[...]
    out[4, 0:4, :] = jnp.where(strip > 0, above, 0.0)
    out[4, 4:8, :] = jnp.where(strip < STRIPS - 1, below, 0.0)


def local_part(near_pair, conductivity, own, swap_a, swap_b, kernel_hbm, rounded, full, around, kernels, sems):
    start_near(kernel_hbm, kernels, sems)
    _, blk = place()
    even = lax.rem(blk, 2) == 0
    left = jnp.where(blk > 0, jnp.where(even, swap_b[...], swap_a[...]), 0.0)
    right = jnp.where(blk < BLKS - 1, jnp.where(even, swap_a[...], swap_b[...]), 0.0)
    for column, blocks in enumerate((left, own[...], right)):
        base = 10 * column
        around[:, base + 1 : base + 9, :] = blocks[0:4]
        around[:, base, :] = blocks[4, 0:4]
        around[:, base + 9, :] = blocks[4, 4:8]
    flux_sum = flux(around, conductivity)
    rounded[3] = flux_sum
    full[3] = flux_sum
    near_rounded, near_full = near(around, near_pair, kernels, lambda n: near_copy(kernel_hbm, kernels, sems, n).wait())
    for a in range(3):
        rounded[a] = near_rounded[:, a * LEN : (a + 1) * LEN]
        full[a] = near_full[:, a * LEN : (a + 1) * LEN]


def first_image(vector, local, received, image, far_part, to_even, to_odd):
    arrived = far_sum(received, lambda g: received[g, 3:4, :])
    for a in range(3):
        far_part[a] = arrived[a]
    own = [vector[c] for c in range(4)]
    result = image_of(own, local, arrived)
    for c in range(4):
        image[c] = result[c]
    strip, _ = place()
    even = lax.rem(strip, 2) == 0
    to_even[...] = jnp.where(even, image[:, ROWS - 1, :], image[:, 0, :])
    to_odd[...] = jnp.where(even, image[:, 0, :], image[:, ROWS - 1, :])


def second_image(vector, image, local_one, local_two, target, received, far_one, first, image_two, scalars, rows):
    vv, vi, ii = totals(received[:, 3, :], 3)
    h = over_entries(vi)
    h0 = h[0]
    h0_pair = (h0, jnp.zeros_like(h0))
    square = pair_add(ii, pair_add(scaled(neg(pair_mul(h0_pair, vi)), 2.0), pair_mul(pair_mul(h0_pair, h0_pair), vv)))
    beta1 = jnp.sqrt(jnp.maximum(square[0], 0.0) / ENTRIES + EPSILON)
    h0_wide = jnp.broadcast_to(h0, (8, LEN))
    beta_wide = jnp.broadcast_to(beta1, (8, LEN))

    def of_first(of_image, of_vector):
        return (of_image - h0_wide * of_vector) / beta_wide

    start = [vector[c] for c in range(4)]
    own = [of_first(image[c], start[c]) for c in range(4)]
    for c in range(4):
        first[c] = own[c]
    arrived = far_sum(received, lambda g: target[g, 3:4, :])
    far_part = [of_first(arrived[a], far_one[a]) for a in range(3)]
    local = [of_first(local_two[c], local_one[c]) for c in range(4)]
    result = image_of(own, local, far_part)
    for c in range(4):
        image_two[c] = result[c]
    row = dot_row([(start, result), (own, result), (result, result), (start, start), (start, own), (own, own)])
    rows[...] = jnp.broadcast_to(row, (DEVICES, LEN))
    lane = lax.broadcasted_iota(jnp.int32, (1, LEN), 1)
    scalars[...] = jnp.where(lane == 0, h0, beta1)


def finish(vector, first, image, scalars, rows, krylov, hessenberg):
    si, fi, ii, ss, sf, ff = totals(rows[...], 6)
    g0, g1 = over_entries(si)[0], over_entries(fi)[0]
    zero = jnp.zeros_like(g0)
    p0, p1 = (g0, zero), (g1, zero)
    square = pair_add(ii, scaled(neg(pair_add(pair_mul(p0, si), pair_mul(p1, fi))), 2.0))
    cross = scaled(pair_mul(pair_mul(p0, p1), sf), 2.0)
    square = pair_add(square, pair_add(cross, pair_add(pair_mul(pair_mul(p0, p0), ss), pair_mul(pair_mul(p1, p1), ff))))
    beta2 = jnp.sqrt(jnp.maximum(square[0], 0.0) / ENTRIES + EPSILON)
    g0_wide, g1_wide, beta_wide = (jnp.broadcast_to(x, (8, LEN)) for x in (g0, g1, beta2))
    for c in range(4):
        krylov[0, c] = first[c]
        krylov[1, c] = (image[c] - g0_wide * vector[c] - g1_wide * first[c]) / beta_wide
    for i, value in enumerate((scalars[0, 0], scalars[0, 1], g0[0, 0], g1[0, 0], beta2[0, 0])):
        hessenberg[i] = value


def shape(*dims):
    return jax.ShapeDtypeStruct(dims, F32)


def limit(mib):
    return pltpu.CompilerParams(vmem_limit_bytes=mib * 1024 * 1024)


def in_hbm(x):
    return pltpu.with_memory_space_constraint(x, pltpu.HBM)


def exchange(x):
    return lax.all_to_all(x, ("strip", "blk"), 0, 0, tiled=True)


def swaps(x, axis, size):
    even = [(i, i ^ 1) for i in range(size)]
    odd = [(i, (i + 1) % size if i % 2 else (i - 1) % size) for i in range(size)]
    return lax.ppermute(x, axis, even), lax.ppermute(x, axis, odd)


def own_blocks(in_vmem, swap_a, swap_b, after):
    return pl.pallas_call(
        edges,
        out_shape=shape(5, ROWS, LEN),
        in_specs=[VMEM] * 3 + [ANY],
        out_specs=VMEM,
        compiler_params=limit(4),
        name="edges",
    )(in_vmem, swap_a, swap_b, after)


def local(vector, conductivity, near_kernel, near_pair, far_right, far_left, far_source_row, far_target_row):
    right = in_hbm(jnp.transpose(far_right[0], (0, 2, 1, 3)))
    left = in_hbm(jnp.transpose(far_left[0], (0, 2, 1, 3)))
    near_kernel = in_hbm(near_kernel)
    source_row, target_row = in_hbm(far_source_row), in_hbm(far_target_row)
    block, slots, line = shape(4, ROWS, LEN), shape(DEVICES, 4, LEN), shape(1, LEN)

    factors = jax.ShapeDtypeStruct((DEVICES, 3, RANK, LEN), BF16)
    integers = jax.ShapeDtypeStruct((1, LEN), jnp.int32)
    cost = pl.CostEstimate(flops=2 * 10**8, bytes_accessed=10**7, transcendentals=0)

    def gathered_and_coefficients(parts):
        gathered = pltpu.VMEM((DEVICES, parts * 3 * LEN), BF16)
        return gathered, jax.ShapeDtypeStruct((FAR_CHUNKS, parts * FAR_CHUNK, FAR_CHUNK * RANK), BF16)

    expand_call = functools.partial(
        pl.pallas_call,
        out_shape=pltpu.HBM(slots.shape, F32),
        in_specs=[VMEM, ANY, VMEM, VMEM],
        out_specs=HBM,
        scratch_shapes=[pltpu.VMEM(slots.shape, F32), pltpu.SemaphoreType.DMA((FAR_COPIES,))],
        compiler_params=limit(4),
        cost_estimate=cost,
    )

    local_call = functools.partial(
        pl.pallas_call,
        local_part,
        out_shape=(block, block),
        in_specs=[SMEM, VMEM, VMEM, VMEM, VMEM, HBM],
        out_specs=(VMEM, VMEM),
        scratch_shapes=[
            pltpu.VMEM((4, HALO, LEN), F32),
            pltpu.VMEM((PAIRS, 3, 3, LEN, LEN), BF16),
            pltpu.SemaphoreType.DMA((NEAR_CHUNKS,)),
        ],
        compiler_params=limit(20),
        cost_estimate=pl.CostEstimate(flops=4 * 10**8, bytes_accessed=2 * 10**7, transcendentals=0),
        name="local_part",
    )

    swapped = swaps(vector, "strip", STRIPS)
    vector_vmem, source_row, target_row, right_vmem = pl.pallas_call(
        bring,
        out_shape=(block, integers, integers, factors),
        in_specs=[HBM] * 4,
        out_specs=(VMEM,) * 4,
        scratch_shapes=[pltpu.SemaphoreType.DMA((4,))],
        compiler_params=limit(4),
        cost_estimate=cost,
        name="bring",
    )(source_row, target_row, in_hbm(vector), right)
    start = own_blocks(vector_vmem, *swapped, source_row)
    sides = swaps(start, "blk", BLKS)
    gathered, coefficients = gathered_and_coefficients(1)
    coefficients, left = pl.pallas_call(
        first_project,
        out_shape=(coefficients, factors),
        in_specs=[VMEM, VMEM, VMEM, HBM],
        out_specs=(VMEM, VMEM),
        scratch_shapes=[gathered, pltpu.SemaphoreType.DMA],
        compiler_params=limit(4),
        cost_estimate=cost,
        name="first_project",
    )(source_row, start, right_vmem, left)
    payload = expand_call(first_expand, name="first_expand")(target_row, start, coefficients, left)
    payload, *sides = lax.optimization_barrier((payload, *sides))
    received_one = exchange(payload)
    rounded_one, local_one = local_call()(near_pair, conductivity, start, *sides, near_kernel)
    image, far_one, to_even, to_odd = pl.pallas_call(
        first_image,
        out_shape=(block, shape(3, ROWS, LEN), shape(4, LEN), shape(4, LEN)),
        in_specs=[VMEM] * 3,
        out_specs=(VMEM,) * 4,
        compiler_params=limit(4),
        name="first_image",
    )(start, rounded_one, received_one)
    swapped = swaps(to_even, "strip", STRIPS)[0], swaps(to_odd, "strip", STRIPS)[1]
    right_vmem = pl.pallas_call(
        bring_right,
        out_shape=factors,
        in_specs=[ANY, HBM],
        out_specs=VMEM,
        scratch_shapes=[pltpu.SemaphoreType.DMA],
        compiler_params=limit(4),
        cost_estimate=cost,
        name="bring_right",
    )(image, right)
    own = own_blocks(image, *swapped, right_vmem)
    sides = swaps(own, "blk", BLKS)
    gathered, coefficients = gathered_and_coefficients(3)
    coefficients = pl.pallas_call(
        second_project,
        out_shape=coefficients,
        in_specs=[VMEM] * 3,
        out_specs=VMEM,
        scratch_shapes=[gathered],
        compiler_params=limit(4),
        cost_estimate=cost,
        name="second_project",
    )(source_row, own, right_vmem)
    payload = expand_call(second_expand, in_specs=[VMEM] * 4, name="second_expand")(start, own, coefficients, left)
    payload, *sides = lax.optimization_barrier((payload, *sides))
    received_two = exchange(payload)
    _, local_two = local_call()(near_pair, conductivity, own, *sides, near_kernel)
    first, image_two, scalars, rows = pl.pallas_call(
        second_image,
        out_shape=(block, block, line, shape(DEVICES, LEN)),
        in_specs=[VMEM] * 7,
        out_specs=(VMEM,) * 4,
        compiler_params=limit(4),
        name="second_image",
    )(start, image, local_one, local_two, received_one, received_two, far_one)
    rows = exchange(rows)
    krylov, hessenberg = pl.pallas_call(
        finish,
        out_shape=(shape(2, 4, ROWS, LEN), shape(5)),
        in_specs=[VMEM] * 5,
        out_specs=(VMEM, SMEM),
        compiler_params=limit(4),
        name="finish",
    )(start, first, image_two, scalars, rows)
    return krylov, hessenberg


def solution(mesh):
    in_specs = (
        P(None, "strip", "blk"),
        P(None, "strip", "blk"),
        P(("strip", "blk"), None, None, None, None),
        P(("strip", "blk")),
        P(("strip", "blk"), None, None, None, None),
        P(("strip", "blk"), None, None, None, None),
        P(("strip", "blk"), None),
        P(("strip", "blk"), None),
    )
    out_specs = (P(None, None, "strip", "blk"), P())
    return jax.shard_map(local, mesh=mesh, in_specs=in_specs, out_specs=out_specs, check_vma=False)
```

```python
import functools

import jax
import jax.numpy as jnp
from jax import lax
from jax.experimental import pallas as pl
from jax.experimental.pallas import tpu as pltpu
from jax.sharding import PartitionSpec as P

EPSILON = 1e-06
STRIPS, BLKS, DEVICES = 8, 16, 128
ROWS, LEN, RANK, PAIRS = 8, 128, 32, 48
ENTRIES = float(4 * STRIPS * ROWS * BLKS * LEN)
HALO = 32
NEAR_CHUNK = 8
NEAR_CHUNKS = PAIRS // NEAR_CHUNK
SMALL_CHUNK = 4
SMALL_CHUNKS = PAIRS // SMALL_CHUNK
FAR_CHUNK = 16
FAR_CHUNKS = DEVICES // FAR_CHUNK
FAR_PER_COPY = 2
FAR_COPIES = FAR_CHUNKS // FAR_PER_COPY
BF16, F32 = jnp.bfloat16, jnp.float32
TRANS_B = (((1,), (1,)), ((), ()))
PLAIN = (((1,), (0,)), ((), ()))
VMEM = pl.BlockSpec(memory_space=pltpu.VMEM)
SMEM = pl.BlockSpec(memory_space=pltpu.SMEM)
ANY = pl.BlockSpec(memory_space=pl.ANY)
HBM = pl.BlockSpec(memory_space=pltpu.HBM)


def two_sum(a, b):
    s = a + b
    t = s - a
    return s, (a - (s - t)) + (b - t)


def halves(a):
    c = a * 4097.0
    hi = c - (c - a)
    return hi, a - hi


def two_prod(a, b):
    p = a * b
    ah, al = halves(a)
    bh, bl = halves(b)
    return p, ((ah * bh - p) + ah * bl + al * bh) + al * bl


def pair_add(x, y):
    s, e = two_sum(x[0], y[0])
    return two_sum(s, e + (x[1] + y[1]))


def loose_add(x, y):
    s, e = two_sum(x[0], y[0])
    return s, e + (x[1] + y[1])


def pair_mul(x, y):
    p, e = two_prod(x[0], y[0])
    return two_sum(p, e + (x[0] * y[1] + x[1] * y[0]))


def neg(x):
    return -x[0], -x[1]


def scaled(x, power_of_two):
    return x[0] * power_of_two, x[1] * power_of_two


def dot_row(pairs):
    sub = lax.broadcasted_iota(jnp.int32, (8, LEN), 0)
    high = jnp.zeros((8, LEN), F32)
    low = jnp.zeros((8, LEN), F32)
    for k, (a, b) in enumerate(pairs):
        s, e = two_prod(a[0], b[0])
        for c in range(1, 4):
            s, e = loose_add((s, e), two_prod(a[c], b[c]))
        for step in (4, 2, 1):
            s, e = loose_add((s, e), (pltpu.roll(s, step, 0), pltpu.roll(e, step, 0)))
        s, e = two_sum(s, e)
        high = jnp.where(sub == k, s, high)
        low = jnp.where(sub == k, e, low)
    pad = jnp.zeros((LEN - 16, LEN), F32)
    turned = jnp.concatenate([high, low, pad], axis=0).T
    s, e = column_sums(turned)
    return s + pltpu.roll(e, 16, 1)


def column_sums(x):
    parts = [(x[8 * i : 8 * i + 8], jnp.zeros((8, LEN), F32)) for i in range(16)]
    while len(parts) > 1:
        parts = [loose_add(parts[i], parts[i + 1]) for i in range(0, len(parts), 2)]
    s, e = parts[0]
    for step in (4, 2, 1):
        s, e = loose_add((s, e), (pltpu.roll(s, step, 0), pltpu.roll(e, step, 0)))
    s, e = two_sum(s[0:1], e[0:1])
    return s, e


def totals(rows, count):
    s, e = column_sums(rows)
    low = e + pltpu.roll(s, LEN - 8, 1) + pltpu.roll(s, LEN - 16, 1)
    s, low = two_sum(s, low)
    return [(s[0:1, k : k + 1], low[0:1, k : k + 1]) for k in range(count)]


def over_entries(x):
    return scaled(x, 1.0 / ENTRIES)


def place():
    strip, blk = lax.axis_index("strip"), lax.axis_index("blk")
    return strip, blk


def near(around, near_pair, kernels, wait):
    sub = lax.broadcasted_iota(jnp.int32, (8, LEN), 0)

    def chunk(n, total):
        wait(n)
        rows, matrices = [], []
        for i in range(NEAR_CHUNK):
            p = n * NEAR_CHUNK + i
            code = near_pair[p]
            t = code // 9
            k = code - 9 * t
            up = k // 3
            source = (k - 3 * up) * 10 + t + up
            for b in range(3):
                rows.append(jnp.where(sub == t, around[b, pl.ds(source, 1), :], 0.0))
                matrices.append(kernels[p, :, b].reshape(3 * LEN, LEN))
        left = jnp.concatenate(split3(jnp.concatenate(rows, axis=1)), axis=0)
        matrix = jnp.concatenate(matrices, axis=1)
        return total + lax.dot_general(left, matrix, TRANS_B, preferred_element_type=F32)

    total = lax.fori_loop(0, NEAR_CHUNKS, chunk, jnp.zeros((24, 3 * LEN), F32))
    return total[0:8], total[0:8] + (total[8:16] + total[16:24])


def near_copy(kernel_hbm, kernels, sems, n, size=NEAR_CHUNK):
    part = pl.ds(n * size, size)
    return pltpu.make_async_copy(kernel_hbm.at[part], kernels.at[part], sems.at[n])


def near_tiles(around, near_pair, kernel_hbm, kernels, sems, tiles):
    def pair(p, carry):
        @pl.when(lax.rem(p, SMALL_CHUNK) == 0)
        def _():
            near_copy(kernel_hbm, kernels, sems, p // SMALL_CHUNK, SMALL_CHUNK).wait()

        code = near_pair[p]
        t = code // 9
        k = code - 9 * t
        up = k // 3
        source = (k - 3 * up) * 10 + t + up
        rows = [around[b, pl.ds(source, 1), :] for b in range(3)]
        for a in range(3):
            for i in range(0, LEN, 16):
                part = pl.ds(i, 16)
                products = [kernels[p, a, b, part, :].astype(F32) * rows[b] for b in range(3)]
                tiles[t, a, part, :] += products[0] + products[1] + products[2]
        return carry

    lax.fori_loop(0, PAIRS, pair, 0)


def lane_sums(tiles, a):
    ones = jnp.ones((8, LEN), BF16)
    pieces = split3(tiles[:, a].reshape(ROWS * LEN, LEN))
    low, mid, high = (lax.dot_general(ones, x, TRANS_B, preferred_element_type=F32) for x in reversed(pieces))
    total = (low + mid) + high
    return jnp.concatenate([total[0:1, t * LEN : (t + 1) * LEN] for t in range(ROWS)], axis=0)


def far_copy(hbm, buffer, sems, n):
    part = pl.ds(n * FAR_CHUNK * FAR_PER_COPY, FAR_CHUNK * FAR_PER_COPY)
    return pltpu.make_async_copy(hbm.at[part], buffer.at[part], sems.at[n])


def split3(x):
    a = x.astype(BF16)
    rest = x - a.astype(F32)
    b = rest.astype(BF16)
    c = (rest - b.astype(F32)).astype(BF16)
    return a, b, c


def own_block():
    sub = lax.broadcasted_iota(jnp.int32, (FAR_CHUNK, FAR_CHUNK * RANK), 0)
    lane = lax.broadcasted_iota(jnp.int32, (FAR_CHUNK, FAR_CHUNK * RANK), 1)
    return lane // RANK == sub


def summed(x, parts):
    if parts == 1:
        return x
    return x[0:FAR_CHUNK] + (x[FAR_CHUNK : 2 * FAR_CHUNK] + x[2 * FAR_CHUNK :])


def project(parts, source_row, vector, coefficients, right, gathered):
    pieces = [[x.astype(BF16)] if parts == 1 else split3(x) for x in (vector[b] for b in range(3))]
    below = jnp.zeros((LEN - ROWS, LEN), F32)
    sources = [jnp.concatenate([pieces[b][k].astype(F32), below], axis=0).astype(BF16) for k in range(parts) for b in range(3)]
    sources = jnp.concatenate(sources, axis=1)
    row = lax.broadcasted_iota(jnp.int32, (LEN, LEN), 0)
    from_row = jnp.where(row == source_row, 1.0, 0.0).T.astype(BF16)
    gathered[...] = lax.dot_general(from_row, sources, PLAIN, preferred_element_type=F32).astype(BF16)
    own = own_block()
    for n in range(FAR_CHUNKS):
        d = pl.ds(n * FAR_CHUNK, FAR_CHUNK)
        source = jnp.concatenate([gathered[d, 3 * LEN * k : 3 * LEN * (k + 1)] for k in range(parts)], axis=0)
        matrix = jnp.concatenate([right[d, b].reshape(FAR_CHUNK * RANK, LEN) for b in range(3)], axis=1)
        c = summed(lax.dot_general(source, matrix, TRANS_B, preferred_element_type=F32), parts)
        c = jnp.where(own, c, 0.0)
        coefficients[n] = c.astype(BF16) if parts == 1 else jnp.concatenate(split3(c), axis=0)


def expand(parts, coefficients, left, out, payload, sems):
    copies = []
    for n in range(FAR_CHUNKS):
        d = pl.ds(n * FAR_CHUNK, FAR_CHUNK)
        matrix = jnp.concatenate([left[d, a].reshape(FAR_CHUNK * RANK, LEN) for a in range(3)], axis=1)
        result = summed(lax.dot_general(coefficients[n], matrix, PLAIN, preferred_element_type=F32), parts)
        for a in range(3):
            payload[d, a, :] = result[:, a * LEN : (a + 1) * LEN]
        if n % FAR_PER_COPY == FAR_PER_COPY - 1:
            copies.append(far_copy(payload, out, sems, n // FAR_PER_COPY))
            copies[-1].start()
    for copy in copies:
        copy.wait()


def far_sum(received, target):
    sub = lax.broadcasted_iota(jnp.int32, (8, LEN), 0).astype(F32)

    def some(n, totals):
        out = list(totals)
        for i in range(8):
            g = n * 8 + i
            hit = target(g) == sub
            for a in range(3):
                k = 3 * (i % 2) + a
                out[k] = out[k] + jnp.where(hit, received[g, a : a + 1, :], 0.0)
        return tuple(out)

    z = lax.fori_loop(0, DEVICES // 8, some, (jnp.zeros((8, LEN), F32),) * 6)
    return [z[a] + z[3 + a] for a in range(3)]


def flux(around, conductivity):
    pressure = around[3, 11:19, :]
    lane = lax.broadcasted_iota(jnp.int32, (8, LEN), 1)
    west = pltpu.roll(jnp.where(lane == LEN - 1, around[3, 1:9, :], pressure), 1, 1)
    east = pltpu.roll(jnp.where(lane == 0, around[3, 21:29, :], pressure), LEN - 1, 1)
    total = conductivity[0] * (around[3, 10:18, :] - pressure) + conductivity[1] * (around[3, 12:20, :] - pressure)
    return total + conductivity[2] * (west - pressure) + conductivity[3] * (east - pressure)


def image_of(vector, local, far_part):
    out = [vector[a] + local[a] + far_part[a] for a in range(3)]
    out[0] = out[0] - vector[3]
    return out + [vector[3] + vector[0] - local[3]]


def start_near(kernel_hbm, kernels, sems):
    for n in range(NEAR_CHUNKS):
        near_copy(kernel_hbm, kernels, sems, n).start()


def bring(source_hbm, target_hbm, vector_hbm, right_hbm, vector, source_row, target_row, right, sems):
    pairs = ((source_hbm, source_row), (vector_hbm, vector), (target_hbm, target_row), (right_hbm, right))
    copies = [pltpu.make_async_copy(x, y, sems.at[i]) for i, (x, y) in enumerate(pairs)]
    for copy in copies:
        copy.start()
    for copy in copies:
        copy.wait()


def bring_right(after, right_hbm, right, sem):
    copy = pltpu.make_async_copy(right_hbm, right, sem)
    copy.start()
    copy.wait()


def first_project(source_row, vector, right, left_hbm, coefficients, left, gathered, sem):
    copy = pltpu.make_async_copy(left_hbm, left, sem)
    copy.start()
    project(1, source_row[...], vector, coefficients, right, gathered)
    copy.wait()


def second_project(source_row, vector, right, coefficients, gathered):
    project(3, source_row[...], vector, coefficients, right, gathered)


def first_expand(target_row, after, coefficients, left, out, payload, sems):
    payload[:, 3, :] = jnp.broadcast_to(target_row[...].astype(F32), (DEVICES, LEN)).T
    expand(1, coefficients, left, out, payload, sems)


def second_expand(vector, image, coefficients, left, out, payload, sems):
    start = [vector[c] for c in range(4)]
    own = [image[c] for c in range(4)]
    row = dot_row([(start, start), (start, own), (own, own)])
    payload[:, 3, :] = jnp.broadcast_to(row, (DEVICES, LEN))
    expand(3, coefficients, left, out, payload, sems)


def edges(vector, swap_a, swap_b, after, out):
    strip, _ = place()
    even = lax.rem(strip, 2) == 0
    if len(swap_a.shape) == 3:
        above = jnp.where(even, swap_b[:, ROWS - 1, :], swap_a[:, ROWS - 1, :])
        below = jnp.where(even, swap_a[:, 0, :], swap_b[:, 0, :])
    else:
        above = jnp.where(even, swap_b[...], swap_a[...])
        below = jnp.where(even, swap_a[...], swap_b[...])
    out[0:4] = vector[...]
    out[4, 0:4, :] = jnp.where(strip > 0, above, 0.0)
    out[4, 4:8, :] = jnp.where(strip < STRIPS - 1, below, 0.0)


def gather_around(around, own, swap_a, swap_b):
    _, blk = place()
    even = lax.rem(blk, 2) == 0
    left = jnp.where(blk > 0, jnp.where(even, swap_b[...], swap_a[...]), 0.0)
    right = jnp.where(blk < BLKS - 1, jnp.where(even, swap_a[...], swap_b[...]), 0.0)
    for column, blocks in enumerate((left, own[...], right)):
        base = 10 * column
        around[:, base + 1 : base + 9, :] = blocks[0:4]
        around[:, base, :] = blocks[4, 0:4]
        around[:, base + 9, :] = blocks[4, 4:8]


def local_part(near_pair, conductivity, own, swap_a, swap_b, kernel_hbm, rounded, full, around, kernels, sems):
    start_near(kernel_hbm, kernels, sems)
    gather_around(around, own, swap_a, swap_b)
    flux_sum = flux(around, conductivity)
    rounded[3] = flux_sum
    full[3] = flux_sum
    near_rounded, near_full = near(around, near_pair, kernels, lambda n: near_copy(kernel_hbm, kernels, sems, n).wait())
    for a in range(3):
        rounded[a] = near_rounded[:, a * LEN : (a + 1) * LEN]
        full[a] = near_full[:, a * LEN : (a + 1) * LEN]


def second_local(
    pair_hbm, conductivity, own, swap_a, swap_b, kernel_hbm, full, around, kernels, sems, near_pair, pair_sem, tiles
):
    pair_copy = pltpu.make_async_copy(pair_hbm, near_pair, pair_sem)
    pair_copy.start()
    for n in range(SMALL_CHUNKS):
        near_copy(kernel_hbm, kernels, sems, n, SMALL_CHUNK).start()
    gather_around(around, own, swap_a, swap_b)
    full[3] = flux(around, conductivity)
    for t in range(ROWS):
        tiles[t] = jnp.zeros((3, LEN, LEN), F32)
    pair_copy.wait()
    near_tiles(around, near_pair, kernel_hbm, kernels, sems, tiles)
    for a in range(3):
        full[a] = lane_sums(tiles, a)


def first_image(vector, local, received, image, far_part, to_even, to_odd):
    arrived = far_sum(received, lambda g: received[g, 3:4, :])
    for a in range(3):
        far_part[a] = arrived[a]
    own = [vector[c] for c in range(4)]
    result = image_of(own, local, arrived)
    for c in range(4):
        image[c] = result[c]
    strip, _ = place()
    even = lax.rem(strip, 2) == 0
    to_even[...] = jnp.where(even, image[:, ROWS - 1, :], image[:, 0, :])
    to_odd[...] = jnp.where(even, image[:, 0, :], image[:, ROWS - 1, :])


def second_image(vector, image, local_one, local_two, target, received, far_one, first, image_two, scalars, rows):
    vv, vi, ii = totals(received[:, 3, :], 3)
    h = over_entries(vi)
    h0 = h[0]
    h0_pair = (h0, jnp.zeros_like(h0))
    square = pair_add(ii, pair_add(scaled(neg(pair_mul(h0_pair, vi)), 2.0), pair_mul(pair_mul(h0_pair, h0_pair), vv)))
    beta1 = jnp.sqrt(jnp.maximum(square[0], 0.0) / ENTRIES + EPSILON)
    h0_wide = jnp.broadcast_to(h0, (8, LEN))
    beta_wide = jnp.broadcast_to(beta1, (8, LEN))

    def of_first(of_image, of_vector):
        return (of_image - h0_wide * of_vector) / beta_wide

    start = [vector[c] for c in range(4)]
    own = [of_first(image[c], start[c]) for c in range(4)]
    for c in range(4):
        first[c] = own[c]
    arrived = far_sum(received, lambda g: target[g, 3:4, :])
    far_part = [of_first(arrived[a], far_one[a]) for a in range(3)]
    local = [of_first(local_two[c], local_one[c]) for c in range(4)]
    result = image_of(own, local, far_part)
    for c in range(4):
        image_two[c] = result[c]
    row = dot_row([(start, result), (own, result), (result, result), (start, start), (start, own), (own, own)])
    rows[...] = jnp.broadcast_to(row, (DEVICES, LEN))
    lane = lax.broadcasted_iota(jnp.int32, (1, LEN), 1)
    scalars[...] = jnp.where(lane == 0, h0, beta1)


def finish(vector, first, image, scalars, rows, krylov, hessenberg):
    si, fi, ii, ss, sf, ff = totals(rows[...], 6)
    g0, g1 = over_entries(si)[0], over_entries(fi)[0]
    zero = jnp.zeros_like(g0)
    p0, p1 = (g0, zero), (g1, zero)
    square = pair_add(ii, scaled(neg(pair_add(pair_mul(p0, si), pair_mul(p1, fi))), 2.0))
    cross = scaled(pair_mul(pair_mul(p0, p1), sf), 2.0)
    square = pair_add(square, pair_add(cross, pair_add(pair_mul(pair_mul(p0, p0), ss), pair_mul(pair_mul(p1, p1), ff))))
    beta2 = jnp.sqrt(jnp.maximum(square[0], 0.0) / ENTRIES + EPSILON)
    g0_wide, g1_wide, beta_wide = (jnp.broadcast_to(x, (8, LEN)) for x in (g0, g1, beta2))
    for c in range(4):
        krylov[0, c] = first[c]
        krylov[1, c] = (image[c] - g0_wide * vector[c] - g1_wide * first[c]) / beta_wide
    for i, value in enumerate((scalars[0, 0], scalars[0, 1], g0[0, 0], g1[0, 0], beta2[0, 0])):
        hessenberg[i] = value


def shape(*dims):
    return jax.ShapeDtypeStruct(dims, F32)


def limit(mib):
    return pltpu.CompilerParams(vmem_limit_bytes=mib * 1024 * 1024)


def in_hbm(x):
    return pltpu.with_memory_space_constraint(x, pltpu.HBM)


def exchange(x):
    return lax.all_to_all(x, ("strip", "blk"), 0, 0, tiled=True)


def swaps(x, axis, size):
    even = [(i, i ^ 1) for i in range(size)]
    odd = [(i, (i + 1) % size if i % 2 else (i - 1) % size) for i in range(size)]
    return lax.ppermute(x, axis, even), lax.ppermute(x, axis, odd)


def own_blocks(in_vmem, swap_a, swap_b, after):
    return pl.pallas_call(
        edges,
        out_shape=shape(5, ROWS, LEN),
        in_specs=[VMEM] * 3 + [ANY],
        out_specs=VMEM,
        compiler_params=limit(4),
        name="edges",
    )(in_vmem, swap_a, swap_b, after)


def local(vector, conductivity, near_kernel, near_pair, far_right, far_left, far_source_row, far_target_row):
    right = in_hbm(jnp.transpose(far_right[0], (0, 2, 1, 3)))
    left = in_hbm(jnp.transpose(far_left[0], (0, 2, 1, 3)))
    near_kernel = in_hbm(near_kernel)
    source_row, target_row = in_hbm(far_source_row), in_hbm(far_target_row)
    block, slots, line = shape(4, ROWS, LEN), shape(DEVICES, 4, LEN), shape(1, LEN)

    factors = jax.ShapeDtypeStruct((DEVICES, 3, RANK, LEN), BF16)
    integers = jax.ShapeDtypeStruct((1, LEN), jnp.int32)
    cost = pl.CostEstimate(flops=2 * 10**8, bytes_accessed=10**7, transcendentals=0)

    def gathered_and_coefficients(parts):
        gathered = pltpu.VMEM((DEVICES, parts * 3 * LEN), BF16)
        return gathered, jax.ShapeDtypeStruct((FAR_CHUNKS, parts * FAR_CHUNK, FAR_CHUNK * RANK), BF16)

    expand_call = functools.partial(
        pl.pallas_call,
        out_shape=pltpu.HBM(slots.shape, F32),
        in_specs=[VMEM, ANY, VMEM, VMEM],
        out_specs=HBM,
        scratch_shapes=[pltpu.VMEM(slots.shape, F32), pltpu.SemaphoreType.DMA((FAR_COPIES,))],
        compiler_params=limit(4),
        cost_estimate=cost,
    )

    local_call = functools.partial(
        pl.pallas_call,
        local_part,
        out_shape=(block, block),
        in_specs=[SMEM, VMEM, VMEM, VMEM, VMEM, HBM],
        out_specs=(VMEM, VMEM),
        scratch_shapes=[
            pltpu.VMEM((4, HALO, LEN), F32),
            pltpu.VMEM((PAIRS, 3, 3, LEN, LEN), BF16),
            pltpu.SemaphoreType.DMA((NEAR_CHUNKS,)),
        ],
        compiler_params=limit(20),
        cost_estimate=pl.CostEstimate(flops=4 * 10**8, bytes_accessed=2 * 10**7, transcendentals=0),
        name="local_part",
    )

    swapped = swaps(vector, "strip", STRIPS)
    vector_vmem, source_row, target_row, right_vmem = pl.pallas_call(
        bring,
        out_shape=(block, integers, integers, factors),
        in_specs=[HBM] * 4,
        out_specs=(VMEM,) * 4,
        scratch_shapes=[pltpu.SemaphoreType.DMA((4,))],
        compiler_params=limit(4),
        cost_estimate=cost,
        name="bring",
    )(source_row, target_row, in_hbm(vector), right)
    start = own_blocks(vector_vmem, *swapped, source_row)
    sides = swaps(start, "blk", BLKS)
    gathered, coefficients = gathered_and_coefficients(1)
    coefficients, left = pl.pallas_call(
        first_project,
        out_shape=(coefficients, factors),
        in_specs=[VMEM, VMEM, VMEM, HBM],
        out_specs=(VMEM, VMEM),
        scratch_shapes=[gathered, pltpu.SemaphoreType.DMA],
        compiler_params=limit(4),
        cost_estimate=cost,
        name="first_project",
    )(source_row, start, right_vmem, left)
    payload = expand_call(first_expand, name="first_expand")(target_row, start, coefficients, left)
    payload, *sides = lax.optimization_barrier((payload, *sides))
    received_one = exchange(payload)
    rounded_one, local_one = local_call()(near_pair, conductivity, start, *sides, near_kernel)
    image, far_one, to_even, to_odd = pl.pallas_call(
        first_image,
        out_shape=(block, shape(3, ROWS, LEN), shape(4, LEN), shape(4, LEN)),
        in_specs=[VMEM] * 3,
        out_specs=(VMEM,) * 4,
        compiler_params=limit(4),
        name="first_image",
    )(start, rounded_one, received_one)
    swapped = swaps(to_even, "strip", STRIPS)[0], swaps(to_odd, "strip", STRIPS)[1]
    right_vmem = pl.pallas_call(
        bring_right,
        out_shape=factors,
        in_specs=[ANY, HBM],
        out_specs=VMEM,
        scratch_shapes=[pltpu.SemaphoreType.DMA],
        compiler_params=limit(4),
        cost_estimate=cost,
        name="bring_right",
    )(image, right)
    own = own_blocks(image, *swapped, right_vmem)
    sides = swaps(own, "blk", BLKS)
    gathered, coefficients = gathered_and_coefficients(3)
    coefficients = pl.pallas_call(
        second_project,
        out_shape=coefficients,
        in_specs=[VMEM] * 3,
        out_specs=VMEM,
        scratch_shapes=[gathered],
        compiler_params=limit(4),
        cost_estimate=cost,
        name="second_project",
    )(source_row, own, right_vmem)
    payload = expand_call(second_expand, in_specs=[VMEM] * 4, name="second_expand")(start, own, coefficients, left)
    payload, *sides = lax.optimization_barrier((payload, *sides))
    received_two = exchange(payload)
    local_two = pl.pallas_call(
        second_local,
        out_shape=block,
        in_specs=[HBM, VMEM, VMEM, VMEM, VMEM, HBM],
        out_specs=VMEM,
        scratch_shapes=[
            pltpu.VMEM((4, HALO, LEN), F32),
            pltpu.VMEM((PAIRS, 3, 3, LEN, LEN), BF16),
            pltpu.SemaphoreType.DMA((SMALL_CHUNKS,)),
            pltpu.SMEM((PAIRS,), jnp.int32),
            pltpu.SemaphoreType.DMA,
            pltpu.VMEM((ROWS, 3, LEN, LEN), F32),
        ],
        compiler_params=limit(24),
        cost_estimate=pl.CostEstimate(flops=4 * 10**8, bytes_accessed=2 * 10**7, transcendentals=0),
        name="second_local",
    )(in_hbm(near_pair), conductivity, own, *sides, near_kernel)
    first, image_two, scalars, rows = pl.pallas_call(
        second_image,
        out_shape=(block, block, line, shape(DEVICES, LEN)),
        in_specs=[VMEM] * 7,
        out_specs=(VMEM,) * 4,
        compiler_params=limit(4),
        name="second_image",
    )(start, image, local_one, local_two, received_one, received_two, far_one)
    rows = exchange(rows)
    krylov, hessenberg = pl.pallas_call(
        finish,
        out_shape=(shape(2, 4, ROWS, LEN), shape(5)),
        in_specs=[VMEM] * 5,
        out_specs=(VMEM, SMEM),
        compiler_params=limit(4),
        name="finish",
    )(start, first, image_two, scalars, rows)
    return krylov, hessenberg


def solution(mesh):
    in_specs = (
        P(None, "strip", "blk"),
        P(None, "strip", "blk"),
        P(("strip", "blk"), None, None, None, None),
        P(("strip", "blk")),
        P(("strip", "blk"), None, None, None, None),
        P(("strip", "blk"), None, None, None, None),
        P(("strip", "blk"), None),
        P(("strip", "blk"), None),
    )
    out_specs = (P(None, None, "strip", "blk"), P())
    return jax.shard_map(local, mesh=mesh, in_specs=in_specs, out_specs=out_specs, check_vma=False)
```

```python
import functools

import jax
import jax.numpy as jnp
from jax import lax
from jax.experimental import pallas as pl
from jax.experimental.pallas import tpu as pltpu
from jax.sharding import PartitionSpec as P

EPSILON = 1e-06
STRIPS, BLKS, DEVICES = 8, 16, 128
ROWS, LEN, RANK, PAIRS = 8, 128, 32, 48
ENTRIES = float(4 * STRIPS * ROWS * BLKS * LEN)
HALO = 32
NEAR_CHUNK = 8
NEAR_CHUNKS = PAIRS // NEAR_CHUNK
SMALL_CHUNK = 4
SMALL_CHUNKS = PAIRS // SMALL_CHUNK
FAR_CHUNK = 16
FAR_CHUNKS = DEVICES // FAR_CHUNK
FAR_PER_COPY = 2
FAR_COPIES = FAR_CHUNKS // FAR_PER_COPY
BF16, F32 = jnp.bfloat16, jnp.float32
TRANS_B = (((1,), (1,)), ((), ()))
PLAIN = (((1,), (0,)), ((), ()))
VMEM = pl.BlockSpec(memory_space=pltpu.VMEM)
SMEM = pl.BlockSpec(memory_space=pltpu.SMEM)
ANY = pl.BlockSpec(memory_space=pl.ANY)
HBM = pl.BlockSpec(memory_space=pltpu.HBM)


def two_sum(a, b):
    s = a + b
    t = s - a
    return s, (a - (s - t)) + (b - t)


def halves(a):
    c = a * 4097.0
    hi = c - (c - a)
    return hi, a - hi


def two_prod(a, b):
    p = a * b
    ah, al = halves(a)
    bh, bl = halves(b)
    return p, ((ah * bh - p) + ah * bl + al * bh) + al * bl


def pair_add(x, y):
    s, e = two_sum(x[0], y[0])
    return two_sum(s, e + (x[1] + y[1]))


def loose_add(x, y):
    s, e = two_sum(x[0], y[0])
    return s, e + (x[1] + y[1])


def pair_mul(x, y):
    p, e = two_prod(x[0], y[0])
    return two_sum(p, e + (x[0] * y[1] + x[1] * y[0]))


def neg(x):
    return -x[0], -x[1]


def scaled(x, power_of_two):
    return x[0] * power_of_two, x[1] * power_of_two


def dot_row(pairs):
    sub = lax.broadcasted_iota(jnp.int32, (8, LEN), 0)
    high = jnp.zeros((8, LEN), F32)
    low = jnp.zeros((8, LEN), F32)
    for k, (a, b) in enumerate(pairs):
        s, e = two_prod(a[0], b[0])
        for c in range(1, 4):
            s, e = loose_add((s, e), two_prod(a[c], b[c]))
        for step in (4, 2, 1):
            s, e = loose_add((s, e), (pltpu.roll(s, step, 0), pltpu.roll(e, step, 0)))
        s, e = two_sum(s, e)
        high = jnp.where(sub == k, s, high)
        low = jnp.where(sub == k, e, low)
    pad = jnp.zeros((LEN - 16, LEN), F32)
    turned = jnp.concatenate([high, low, pad], axis=0).T
    s, e = column_sums(turned)
    return s + pltpu.roll(e, 16, 1)


def column_sums(x):
    parts = [(x[8 * i : 8 * i + 8], jnp.zeros((8, LEN), F32)) for i in range(16)]
    while len(parts) > 1:
        parts = [loose_add(parts[i], parts[i + 1]) for i in range(0, len(parts), 2)]
    s, e = parts[0]
    for step in (4, 2, 1):
        s, e = loose_add((s, e), (pltpu.roll(s, step, 0), pltpu.roll(e, step, 0)))
    s, e = two_sum(s[0:1], e[0:1])
    return s, e


def totals(rows, count):
    s, e = column_sums(rows)
    low = e + pltpu.roll(s, LEN - 8, 1) + pltpu.roll(s, LEN - 16, 1)
    s, low = two_sum(s, low)
    return [(s[0:1, k : k + 1], low[0:1, k : k + 1]) for k in range(count)]


def over_entries(x):
    return scaled(x, 1.0 / ENTRIES)


def place():
    strip, blk = lax.axis_index("strip"), lax.axis_index("blk")
    return strip, blk


def near(around, near_pair, kernels, wait):
    sub = lax.broadcasted_iota(jnp.int32, (8, LEN), 0)

    def chunk(n, total):
        wait(n)
        rows, matrices = [], []
        for i in range(NEAR_CHUNK):
            p = n * NEAR_CHUNK + i
            code = near_pair[p]
            t = code // 9
            k = code - 9 * t
            up = k // 3
            source = (k - 3 * up) * 10 + t + up
            for b in range(3):
                rows.append(jnp.where(sub == t, around[b, pl.ds(source, 1), :], 0.0))
                matrices.append(kernels[p, :, b].reshape(3 * LEN, LEN))
        left = jnp.concatenate(split3(jnp.concatenate(rows, axis=1))[:2], axis=0)
        matrix = jnp.concatenate(matrices, axis=1)
        return total + lax.dot_general(left, matrix, TRANS_B, preferred_element_type=F32)

    total = lax.fori_loop(0, NEAR_CHUNKS, chunk, jnp.zeros((16, 3 * LEN), F32))
    return total[0:8], total[0:8] + total[8:16]


def near_copy(kernel_hbm, kernels, sems, n, size=NEAR_CHUNK):
    part = pl.ds(n * size, size)
    return pltpu.make_async_copy(kernel_hbm.at[part], kernels.at[part], sems.at[n])


def near_tiles(around, near_pair, kernel_hbm, kernels, sems, tiles):
    def pair(p, carry):
        @pl.when(lax.rem(p, SMALL_CHUNK) == 0)
        def _():
            near_copy(kernel_hbm, kernels, sems, p // SMALL_CHUNK, SMALL_CHUNK).wait()

        code = near_pair[p]
        t = code // 9
        k = code - 9 * t
        up = k // 3
        source = (k - 3 * up) * 10 + t + up
        rows = [around[b, pl.ds(source, 1), :] for b in range(3)]
        for a in range(3):
            for i in range(0, LEN, 16):
                part = pl.ds(i, 16)
                products = [kernels[p, a, b, part, :].astype(F32) * rows[b] for b in range(3)]
                tiles[t, a, part, :] += products[0] + products[1] + products[2]
        return carry

    lax.fori_loop(0, PAIRS, pair, 0)


def lane_sums(tiles, a):
    ones = jnp.ones((8, LEN), BF16)
    pieces = split3(tiles[:, a].reshape(ROWS * LEN, LEN))
    low, mid, high = (lax.dot_general(ones, x, TRANS_B, preferred_element_type=F32) for x in reversed(pieces))
    total = (low + mid) + high
    return jnp.concatenate([total[0:1, t * LEN : (t + 1) * LEN] for t in range(ROWS)], axis=0)


def far_copy(hbm, buffer, sems, n):
    part = pl.ds(n * FAR_CHUNK * FAR_PER_COPY, FAR_CHUNK * FAR_PER_COPY)
    return pltpu.make_async_copy(hbm.at[part], buffer.at[part], sems.at[n])


def split3(x):
    a = x.astype(BF16)
    rest = x - a.astype(F32)
    b = rest.astype(BF16)
    c = (rest - b.astype(F32)).astype(BF16)
    return a, b, c


def own_block():
    sub = lax.broadcasted_iota(jnp.int32, (FAR_CHUNK, FAR_CHUNK * RANK), 0)
    lane = lax.broadcasted_iota(jnp.int32, (FAR_CHUNK, FAR_CHUNK * RANK), 1)
    return lane // RANK == sub


def summed(x, parts):
    if parts == 1:
        return x
    return x[0:FAR_CHUNK] + (x[FAR_CHUNK : 2 * FAR_CHUNK] + x[2 * FAR_CHUNK :])


def project(parts, source_row, vector, coefficients, right, gathered):
    pieces = [[x.astype(BF16)] if parts == 1 else split3(x) for x in (vector[b] for b in range(3))]
    below = jnp.zeros((LEN - ROWS, LEN), F32)
    sources = [jnp.concatenate([pieces[b][k].astype(F32), below], axis=0).astype(BF16) for k in range(parts) for b in range(3)]
    sources = jnp.concatenate(sources, axis=1)
    row = lax.broadcasted_iota(jnp.int32, (LEN, LEN), 0)
    from_row = jnp.where(row == source_row, 1.0, 0.0).T.astype(BF16)
    gathered[...] = lax.dot_general(from_row, sources, PLAIN, preferred_element_type=F32).astype(BF16)
    own = own_block()
    for n in range(FAR_CHUNKS):
        d = pl.ds(n * FAR_CHUNK, FAR_CHUNK)
        source = jnp.concatenate([gathered[d, 3 * LEN * k : 3 * LEN * (k + 1)] for k in range(parts)], axis=0)
        matrix = jnp.concatenate([right[d, b].reshape(FAR_CHUNK * RANK, LEN) for b in range(3)], axis=1)
        c = summed(lax.dot_general(source, matrix, TRANS_B, preferred_element_type=F32), parts)
        c = jnp.where(own, c, 0.0)
        coefficients[n] = c.astype(BF16) if parts == 1 else jnp.concatenate(split3(c), axis=0)


def expand(parts, coefficients, left, out, payload, sems):
    copies = []
    for n in range(FAR_CHUNKS):
        d = pl.ds(n * FAR_CHUNK, FAR_CHUNK)
        matrix = jnp.concatenate([left[d, a].reshape(FAR_CHUNK * RANK, LEN) for a in range(3)], axis=1)
        result = summed(lax.dot_general(coefficients[n], matrix, PLAIN, preferred_element_type=F32), parts)
        for a in range(3):
            payload[d, a, :] = result[:, a * LEN : (a + 1) * LEN]
        if n % FAR_PER_COPY == FAR_PER_COPY - 1:
            copies.append(far_copy(payload, out, sems, n // FAR_PER_COPY))
            copies[-1].start()
    for copy in copies:
        copy.wait()


def far_sum(received, target):
    sub = lax.broadcasted_iota(jnp.int32, (8, LEN), 0).astype(F32)

    def some(n, totals):
        out = list(totals)
        for i in range(8):
            g = n * 8 + i
            hit = target(g) == sub
            for a in range(3):
                k = 3 * (i % 2) + a
                out[k] = out[k] + jnp.where(hit, received[g, a : a + 1, :], 0.0)
        return tuple(out)

    z = lax.fori_loop(0, DEVICES // 8, some, (jnp.zeros((8, LEN), F32),) * 6)
    return [z[a] + z[3 + a] for a in range(3)]


def flux(around, conductivity):
    pressure = around[3, 11:19, :]
    lane = lax.broadcasted_iota(jnp.int32, (8, LEN), 1)
    west = pltpu.roll(jnp.where(lane == LEN - 1, around[3, 1:9, :], pressure), 1, 1)
    east = pltpu.roll(jnp.where(lane == 0, around[3, 21:29, :], pressure), LEN - 1, 1)
    total = conductivity[0] * (around[3, 10:18, :] - pressure) + conductivity[1] * (around[3, 12:20, :] - pressure)
    return total + conductivity[2] * (west - pressure) + conductivity[3] * (east - pressure)


def image_of(vector, local, far_part):
    out = [vector[a] + local[a] + far_part[a] for a in range(3)]
    out[0] = out[0] - vector[3]
    return out + [vector[3] + vector[0] - local[3]]


def start_near(kernel_hbm, kernels, sems):
    for n in range(NEAR_CHUNKS):
        near_copy(kernel_hbm, kernels, sems, n).start()


def bring(source_hbm, target_hbm, vector_hbm, right_hbm, vector, source_row, target_row, right, sems):
    pairs = ((source_hbm, source_row), (vector_hbm, vector), (target_hbm, target_row), (right_hbm, right))
    copies = [pltpu.make_async_copy(x, y, sems.at[i]) for i, (x, y) in enumerate(pairs)]
    for copy in copies:
        copy.start()
    for copy in copies:
        copy.wait()


def bring_right(after, right_hbm, right, sem):
    copy = pltpu.make_async_copy(right_hbm, right, sem)
    copy.start()
    copy.wait()


def first_project(source_row, vector, right, left_hbm, coefficients, left, gathered, sem):
    copy = pltpu.make_async_copy(left_hbm, left, sem)
    copy.start()
    project(1, source_row[...], vector, coefficients, right, gathered)
    copy.wait()


def second_project(source_row, vector, right, coefficients, gathered):
    project(3, source_row[...], vector, coefficients, right, gathered)


def first_expand(target_row, after, coefficients, left, out, payload, sems):
    payload[:, 3, :] = jnp.broadcast_to(target_row[...].astype(F32), (DEVICES, LEN)).T
    expand(1, coefficients, left, out, payload, sems)


def second_expand(vector, image, coefficients, left, out, payload, sems):
    start = [vector[c] for c in range(4)]
    own = [image[c] for c in range(4)]
    row = dot_row([(start, start), (start, own), (own, own)])
    payload[:, 3, :] = jnp.broadcast_to(row, (DEVICES, LEN))
    expand(3, coefficients, left, out, payload, sems)


def edges(vector, swap_a, swap_b, after, out):
    strip, _ = place()
    even = lax.rem(strip, 2) == 0
    if len(swap_a.shape) == 3:
        above = jnp.where(even, swap_b[:, ROWS - 1, :], swap_a[:, ROWS - 1, :])
        below = jnp.where(even, swap_a[:, 0, :], swap_b[:, 0, :])
    else:
        above = jnp.where(even, swap_b[...], swap_a[...])
        below = jnp.where(even, swap_a[...], swap_b[...])
    out[0:4] = vector[...]
    out[4, 0:4, :] = jnp.where(strip > 0, above, 0.0)
    out[4, 4:8, :] = jnp.where(strip < STRIPS - 1, below, 0.0)


def gather_around(around, own, swap_a, swap_b):
    _, blk = place()
    even = lax.rem(blk, 2) == 0
    left = jnp.where(blk > 0, jnp.where(even, swap_b[...], swap_a[...]), 0.0)
    right = jnp.where(blk < BLKS - 1, jnp.where(even, swap_a[...], swap_b[...]), 0.0)
    for column, blocks in enumerate((left, own[...], right)):
        base = 10 * column
        around[:, base + 1 : base + 9, :] = blocks[0:4]
        around[:, base, :] = blocks[4, 0:4]
        around[:, base + 9, :] = blocks[4, 4:8]


def local_part(near_pair, conductivity, own, swap_a, swap_b, kernel_hbm, rounded, full, around, kernels, sems):
    start_near(kernel_hbm, kernels, sems)
    gather_around(around, own, swap_a, swap_b)
    flux_sum = flux(around, conductivity)
    rounded[3] = flux_sum
    full[3] = flux_sum
    near_rounded, near_full = near(around, near_pair, kernels, lambda n: near_copy(kernel_hbm, kernels, sems, n).wait())
    for a in range(3):
        rounded[a] = near_rounded[:, a * LEN : (a + 1) * LEN]
        full[a] = near_full[:, a * LEN : (a + 1) * LEN]


def second_local(
    pair_hbm, conductivity, own, swap_a, swap_b, kernel_hbm, full, around, kernels, sems, near_pair, pair_sem, tiles
):
    pair_copy = pltpu.make_async_copy(pair_hbm, near_pair, pair_sem)
    pair_copy.start()
    for n in range(SMALL_CHUNKS):
        near_copy(kernel_hbm, kernels, sems, n, SMALL_CHUNK).start()
    gather_around(around, own, swap_a, swap_b)
    full[3] = flux(around, conductivity)
    for t in range(ROWS):
        tiles[t] = jnp.zeros((3, LEN, LEN), F32)
    pair_copy.wait()
    near_tiles(around, near_pair, kernel_hbm, kernels, sems, tiles)
    for a in range(3):
        full[a] = lane_sums(tiles, a)


def first_image(vector, local, received, image, far_part, to_even, to_odd):
    arrived = far_sum(received, lambda g: received[g, 3:4, :])
    for a in range(3):
        far_part[a] = arrived[a]
    own = [vector[c] for c in range(4)]
    result = image_of(own, local, arrived)
    for c in range(4):
        image[c] = result[c]
    strip, _ = place()
    even = lax.rem(strip, 2) == 0
    to_even[...] = jnp.where(even, image[:, ROWS - 1, :], image[:, 0, :])
    to_odd[...] = jnp.where(even, image[:, 0, :], image[:, ROWS - 1, :])


def second_image(vector, image, local_one, local_two, target, received, far_one, first, image_two, scalars, rows):
    vv, vi, ii = totals(received[:, 3, :], 3)
    h = over_entries(vi)
    h0 = h[0]
    h0_pair = (h0, jnp.zeros_like(h0))
    square = pair_add(ii, pair_add(scaled(neg(pair_mul(h0_pair, vi)), 2.0), pair_mul(pair_mul(h0_pair, h0_pair), vv)))
    beta1 = jnp.sqrt(jnp.maximum(square[0], 0.0) / ENTRIES + EPSILON)
    h0_wide = jnp.broadcast_to(h0, (8, LEN))
    beta_wide = jnp.broadcast_to(beta1, (8, LEN))

    def of_first(of_image, of_vector):
        return (of_image - h0_wide * of_vector) / beta_wide

    start = [vector[c] for c in range(4)]
    own = [of_first(image[c], start[c]) for c in range(4)]
    for c in range(4):
        first[c] = own[c]
    arrived = far_sum(received, lambda g: target[g, 3:4, :])
    far_part = [of_first(arrived[a], far_one[a]) for a in range(3)]
    local = [of_first(local_two[c], local_one[c]) for c in range(4)]
    result = image_of(own, local, far_part)
    for c in range(4):
        image_two[c] = result[c]
    row = dot_row([(start, result), (own, result), (result, result), (start, start), (start, own), (own, own)])
    rows[...] = jnp.broadcast_to(row, (DEVICES, LEN))
    lane = lax.broadcasted_iota(jnp.int32, (1, LEN), 1)
    scalars[...] = jnp.where(lane == 0, h0, beta1)


def finish(vector, first, image, scalars, rows, krylov, hessenberg):
    si, fi, ii, ss, sf, ff = totals(rows[...], 6)
    g0, g1 = over_entries(si)[0], over_entries(fi)[0]
    zero = jnp.zeros_like(g0)
    p0, p1 = (g0, zero), (g1, zero)
    square = pair_add(ii, scaled(neg(pair_add(pair_mul(p0, si), pair_mul(p1, fi))), 2.0))
    cross = scaled(pair_mul(pair_mul(p0, p1), sf), 2.0)
    square = pair_add(square, pair_add(cross, pair_add(pair_mul(pair_mul(p0, p0), ss), pair_mul(pair_mul(p1, p1), ff))))
    beta2 = jnp.sqrt(jnp.maximum(square[0], 0.0) / ENTRIES + EPSILON)
    g0_wide, g1_wide, beta_wide = (jnp.broadcast_to(x, (8, LEN)) for x in (g0, g1, beta2))
    for c in range(4):
        krylov[0, c] = first[c]
        krylov[1, c] = (image[c] - g0_wide * vector[c] - g1_wide * first[c]) / beta_wide
    for i, value in enumerate((scalars[0, 0], scalars[0, 1], g0[0, 0], g1[0, 0], beta2[0, 0])):
        hessenberg[i] = value


def shape(*dims):
    return jax.ShapeDtypeStruct(dims, F32)


def limit(mib):
    return pltpu.CompilerParams(vmem_limit_bytes=mib * 1024 * 1024)


def in_hbm(x):
    return pltpu.with_memory_space_constraint(x, pltpu.HBM)


def exchange(x):
    return lax.all_to_all(x, ("strip", "blk"), 0, 0, tiled=True)


def swaps(x, axis, size):
    even = [(i, i ^ 1) for i in range(size)]
    odd = [(i, (i + 1) % size if i % 2 else (i - 1) % size) for i in range(size)]
    return lax.ppermute(x, axis, even), lax.ppermute(x, axis, odd)


def own_blocks(in_vmem, swap_a, swap_b, after):
    return pl.pallas_call(
        edges,
        out_shape=shape(5, ROWS, LEN),
        in_specs=[VMEM] * 3 + [ANY],
        out_specs=VMEM,
        compiler_params=limit(4),
        name="edges",
    )(in_vmem, swap_a, swap_b, after)


def local(vector, conductivity, near_kernel, near_pair, far_right, far_left, far_source_row, far_target_row):
    right = in_hbm(jnp.transpose(far_right[0], (0, 2, 1, 3)))
    left = in_hbm(jnp.transpose(far_left[0], (0, 2, 1, 3)))
    near_kernel = in_hbm(near_kernel)
    source_row, target_row = in_hbm(far_source_row), in_hbm(far_target_row)
    block, slots, line = shape(4, ROWS, LEN), shape(DEVICES, 4, LEN), shape(1, LEN)

    factors = jax.ShapeDtypeStruct((DEVICES, 3, RANK, LEN), BF16)
    integers = jax.ShapeDtypeStruct((1, LEN), jnp.int32)
    cost = pl.CostEstimate(flops=2 * 10**8, bytes_accessed=10**7, transcendentals=0)

    def gathered_and_coefficients(parts):
        gathered = pltpu.VMEM((DEVICES, parts * 3 * LEN), BF16)
        return gathered, jax.ShapeDtypeStruct((FAR_CHUNKS, parts * FAR_CHUNK, FAR_CHUNK * RANK), BF16)

    expand_call = functools.partial(
        pl.pallas_call,
        out_shape=pltpu.HBM(slots.shape, F32),
        in_specs=[VMEM, ANY, VMEM, VMEM],
        out_specs=HBM,
        scratch_shapes=[pltpu.VMEM(slots.shape, F32), pltpu.SemaphoreType.DMA((FAR_COPIES,))],
        compiler_params=limit(4),
        cost_estimate=cost,
    )

    local_call = functools.partial(
        pl.pallas_call,
        local_part,
        out_shape=(block, block),
        in_specs=[SMEM, VMEM, VMEM, VMEM, VMEM, HBM],
        out_specs=(VMEM, VMEM),
        scratch_shapes=[
            pltpu.VMEM((4, HALO, LEN), F32),
            pltpu.VMEM((PAIRS, 3, 3, LEN, LEN), BF16),
            pltpu.SemaphoreType.DMA((NEAR_CHUNKS,)),
        ],
        compiler_params=limit(20),
        cost_estimate=pl.CostEstimate(flops=4 * 10**8, bytes_accessed=2 * 10**7, transcendentals=0),
        name="local_part",
    )

    swapped = swaps(vector, "strip", STRIPS)
    vector_vmem, source_row, target_row, right_vmem = pl.pallas_call(
        bring,
        out_shape=(block, integers, integers, factors),
        in_specs=[HBM] * 4,
        out_specs=(VMEM,) * 4,
        scratch_shapes=[pltpu.SemaphoreType.DMA((4,))],
        compiler_params=limit(4),
        cost_estimate=cost,
        name="bring",
    )(source_row, target_row, in_hbm(vector), right)
    start = own_blocks(vector_vmem, *swapped, source_row)
    sides = swaps(start, "blk", BLKS)
    gathered, coefficients = gathered_and_coefficients(1)
    coefficients, left = pl.pallas_call(
        first_project,
        out_shape=(coefficients, factors),
        in_specs=[VMEM, VMEM, VMEM, HBM],
        out_specs=(VMEM, VMEM),
        scratch_shapes=[gathered, pltpu.SemaphoreType.DMA],
        compiler_params=limit(4),
        cost_estimate=cost,
        name="first_project",
    )(source_row, start, right_vmem, left)
    payload = expand_call(first_expand, name="first_expand")(target_row, start, coefficients, left)
    payload, *sides = lax.optimization_barrier((payload, *sides))
    received_one = exchange(payload)
    rounded_one, local_one = local_call()(near_pair, conductivity, start, *sides, near_kernel)
    image, far_one, to_even, to_odd = pl.pallas_call(
        first_image,
        out_shape=(block, shape(3, ROWS, LEN), shape(4, LEN), shape(4, LEN)),
        in_specs=[VMEM] * 3,
        out_specs=(VMEM,) * 4,
        compiler_params=limit(4),
        name="first_image",
    )(start, rounded_one, received_one)
    swapped = swaps(to_even, "strip", STRIPS)[0], swaps(to_odd, "strip", STRIPS)[1]
    right_vmem = pl.pallas_call(
        bring_right,
        out_shape=factors,
        in_specs=[ANY, HBM],
        out_specs=VMEM,
        scratch_shapes=[pltpu.SemaphoreType.DMA],
        compiler_params=limit(4),
        cost_estimate=cost,
        name="bring_right",
    )(image, right)
    own = own_blocks(image, *swapped, right_vmem)
    sides = swaps(own, "blk", BLKS)
    gathered, coefficients = gathered_and_coefficients(3)
    coefficients = pl.pallas_call(
        second_project,
        out_shape=coefficients,
        in_specs=[VMEM] * 3,
        out_specs=VMEM,
        scratch_shapes=[gathered],
        compiler_params=limit(4),
        cost_estimate=cost,
        name="second_project",
    )(source_row, own, right_vmem)
    payload = expand_call(second_expand, in_specs=[VMEM] * 4, name="second_expand")(start, own, coefficients, left)
    payload, *sides = lax.optimization_barrier((payload, *sides))
    received_two = exchange(payload)
    local_two = pl.pallas_call(
        second_local,
        out_shape=block,
        in_specs=[HBM, VMEM, VMEM, VMEM, VMEM, HBM],
        out_specs=VMEM,
        scratch_shapes=[
            pltpu.VMEM((4, HALO, LEN), F32),
            pltpu.VMEM((PAIRS, 3, 3, LEN, LEN), BF16),
            pltpu.SemaphoreType.DMA((SMALL_CHUNKS,)),
            pltpu.SMEM((PAIRS,), jnp.int32),
            pltpu.SemaphoreType.DMA,
            pltpu.VMEM((ROWS, 3, LEN, LEN), F32),
        ],
        compiler_params=limit(24),
        cost_estimate=pl.CostEstimate(flops=4 * 10**8, bytes_accessed=2 * 10**7, transcendentals=0),
        name="second_local",
    )(in_hbm(near_pair), conductivity, own, *sides, near_kernel)
    first, image_two, scalars, rows = pl.pallas_call(
        second_image,
        out_shape=(block, block, line, shape(DEVICES, LEN)),
        in_specs=[VMEM] * 7,
        out_specs=(VMEM,) * 4,
        compiler_params=limit(4),
        name="second_image",
    )(start, image, local_one, local_two, received_one, received_two, far_one)
    rows = exchange(rows)
    krylov, hessenberg = pl.pallas_call(
        finish,
        out_shape=(shape(2, 4, ROWS, LEN), shape(5)),
        in_specs=[VMEM] * 5,
        out_specs=(VMEM, SMEM),
        compiler_params=limit(4),
        name="finish",
    )(start, first, image_two, scalars, rows)
    return krylov, hessenberg


def solution(mesh):
    in_specs = (
        P(None, "strip", "blk"),
        P(None, "strip", "blk"),
        P(("strip", "blk"), None, None, None, None),
        P(("strip", "blk")),
        P(("strip", "blk"), None, None, None, None),
        P(("strip", "blk"), None, None, None, None),
        P(("strip", "blk"), None),
        P(("strip", "blk"), None),
    )
    out_specs = (P(None, None, "strip", "blk"), P())
    return jax.shard_map(local, mesh=mesh, in_specs=in_specs, out_specs=out_specs, check_vma=False)
```
